32 devices in a mesh: dp: 4 (over y, x), expert: 8 (over z, core).
Axes of the slice: x: 2, y: 2, z: 4, core: 2. Of those that a mesh axis runs over, the one named last changes fastest.
Arguments:
- tokens: bfloat16 [4096, 2560], P(('dp', 'expert')), may hold values from -6 to 6
- routes: int32 [4096, 2], P(('dp', 'expert')), may hold values from 0 to 7, all different within a row; in each aligned block of 128 rows (0 to 127, 128 to 255, ...) at most 36 rows name the same one
- route_gates: float32 [4096, 2], P(('dp', 'expert')), may hold values from 0.2 to 1
- w_gate: bfloat16 [8, 2560, 768], P('expert', 'dp'), may hold values from -0.125 to 0.125
- w_up: bfloat16 [8, 2560, 768], P('expert', 'dp'), may hold values from -0.125 to 0.125
- w_down: bfloat16 [8, 768, 2560], P('expert', None, 'dp'), may hold values from -0.21875 to 0.21875
- cotangent: bfloat16 [4096, 2560], P(('dp', 'expert')), may hold values from -6 to 6
Outputs:
- layer_out: bfloat16 [4096, 2560], P(('dp', 'expert'))
- token_grad: bfloat16 [4096, 2560], P(('dp', 'expert'))
- gate_grad: float32 [4096, 2], P(('dp', 'expert'))
The draws below stay inside these ranges and needn't reach their ends.
Inputs may be any that keep to these rules, and one draw needn't show every extreme that they name: `routes`: among the 128 rows of one device, each expert is named at most 36 times, and in every draw some device names some expert exactly 36 times. The 2 experts of a token differ.
All inputs are finite; a program needn't handle non-finite values.
Results may differ from the reference program's by a relative error of at most 0.0067.
Values may be sent and summed in bfloat16 or wider, within the bound.
A program may use at most 128 MiB of HBM per device.

```python
import math
import jax
import jax.numpy as jnp
import numpy as np
from jax import lax

D = 2560
FF = 768
TOK_DEV = 128
TOPK = 2
EXPERTS = 8
CAP = 36
TOKENS = 4096


def block_levels(key, dims, shards, smallest, top_value):
    def one(dim, blocks):
        draws = jax.random.uniform(jax.random.fold_in(jax.random.fold_in(key, 6), dim), (blocks,), jnp.float32, smallest / len(shards), top_value / len(shards))
        return jnp.repeat(jnp.exp(draws), dims[dim] // blocks).reshape((-1,) + (1,) * (len(dims) - dim - 1))

    level = one(*shards[0])
    for cut in shards[1:]:
        level = level * one(*cut)
    return level


def deal_out(rng, own, number, rows, amount, top, limit, slope):
    sequence = jax.random.permutation(rng, amount)
    heavy_load, ordinary = portions_of(amount, rows * top, limit, slope, True), portions_of(amount, rows * top, limit, slope, False)
    places = jnp.arange(amount)

    def named(tallies, rotation):
        used = int((tallies > 0).sum())
        fixed = max(1, used // 4)
        passed = fixed + (places - fixed + rotation * (used - fixed)) % max(1, amount - fixed)
        return jnp.zeros((amount,), jnp.int32).at[sequence[jnp.where(places < fixed, places, passed)]].set(jnp.asarray(tallies, jnp.int32))

    tallies = jnp.where(number % 4 == 0, named(heavy_load, number // 4), named(ordinary, number - number // 4 - 1))
    mixed = jax.random.permutation(jax.random.fold_in(own, 3), amount)
    giver, receiver = mixed[0:amount // 2 * 2:2], mixed[1:amount // 2 * 2:2]
    room = jnp.minimum(tallies[giver] - 1, limit - tallies[receiver]) // 2
    room = jnp.where((giver == sequence[0]) | (receiver == sequence[0]) | (tallies[receiver] == 0), 0, jnp.maximum(room, 0))
    passed = jax.random.randint(jax.random.fold_in(own, 4), (amount // 2,), 0, 1 << 20) % (room + 1)
    tallies = tallies.at[giver].add(-passed).at[receiver].add(passed)
    labels = jnp.searchsorted(jnp.cumsum(tallies), jnp.arange(rows * top), side="right").astype(jnp.int32)
    grid = labels.reshape(top, rows).T
    grid = grid[jax.random.permutation(jax.random.fold_in(own, 1), rows)]
    rotation = jax.random.randint(jax.random.fold_in(own, 2), (rows, 1), 0, top)
    return jnp.take_along_axis(grid, (jnp.arange(top)[None, :] + rotation) % top, axis=1)


def portions_of(number_of, total, limit, lean, full):
    portions = [(1 << 20) // math.isqrt(standing ** lean) + 1 for standing in range(1, number_of + 1)]
    largest = limit if full else min(limit, max(-(-total // number_of), total * portions[0] // sum(portions)))
    least = 1 if total - largest >= number_of - 1 else 0
    given, spare = [largest] + [least] * (number_of - 1), total - largest - least * (number_of - 1)
    while spare > 0:
        free = [i for i in range(1, number_of) if given[i] < largest] or [i for i in range(1, number_of) if given[i] < limit]
        pool, budget = sum([portions[i] for i in free]), spare
        for i in free:
            extra = min(limit - given[i], max(1, budget * portions[i] // pool), spare)
            given[i] = given[i] + extra
            spare = spare - extra
    return np.array(given)


def bell_draw(rng, dims, width, bound, pieces=(), kind=jnp.bfloat16):
    values = width * jax.random.normal(rng, dims, jnp.float32)
    if pieces:
        values = values * block_levels(rng, dims, pieces, -0.22, 0.18)
    return jnp.clip(values, -bound, bound).astype(kind)


def setup_inputs(seed: int = 0) -> dict:
    streams_of = jax.random.split(jax.random.key(seed), 8)
    tokens = bell_draw(streams_of[0], (TOKENS, D), 1.0, 6.0, ((0, 32),))
    routes_keys = jax.random.split(jax.random.fold_in(streams_of[1], 1), TOKENS // TOK_DEV)
    routes_turns = jax.random.permutation(jax.random.fold_in(streams_of[1], 3), TOKENS // TOK_DEV)
    routes = jax.vmap(lambda own, number: deal_out(jax.random.fold_in(streams_of[1], 2), own, number, TOK_DEV, EXPERTS, TOPK, CAP, 0))(routes_keys, routes_turns).reshape((TOKENS, TOPK))
    route_gates = jnp.clip(0.2 + 0.8 * jax.random.uniform(streams_of[2], (TOKENS, TOPK), jnp.float32) ** block_levels(streams_of[2], (TOKENS, TOPK), ((0, 32),), -0.2, 0.2), 0.2, 1.0)
    w_gate = bell_draw(streams_of[3], (EXPERTS, D, FF), D ** -0.5, 0.125, ((0, 8), (1, 4)))
    w_up = bell_draw(streams_of[4], (EXPERTS, D, FF), D ** -0.5, 0.125, ((0, 8), (1, 4)))
    w_down = bell_draw(streams_of[5], (EXPERTS, FF, D), FF ** -0.5, 0.21875, ((0, 8), (2, 4)))
    cotangent = bell_draw(streams_of[6], (TOKENS, D), 1.0, 6.0, ((0, 32),))
    return dict(tokens=tokens, routes=routes, route_gates=route_gates, w_gate=w_gate, w_up=w_up, w_down=w_down, cotangent=cotangent)


def expert_pass(rows, cot_rows, gate_rows, gate_mat, up_mat, down_mat):
    gate_pre = jnp.dot(rows, gate_mat, preferred_element_type=jnp.float32)
    up_pre = jnp.dot(rows, up_mat, preferred_element_type=jnp.float32)
    logistic = jax.nn.sigmoid(gate_pre)
    hidden = (gate_pre * logistic * up_pre).astype(jnp.bfloat16)
    expert_out = jnp.dot(hidden, down_mat, preferred_element_type=jnp.float32).astype(jnp.bfloat16)
    row_grad = (gate_rows[:, None] * cot_rows.astype(jnp.float32)).astype(jnp.bfloat16)
    hidden_grad = jnp.dot(row_grad, down_mat.T, preferred_element_type=jnp.float32)
    pre_gate = (hidden_grad * up_pre * logistic * (1.0 + gate_pre * (1.0 - logistic))).astype(jnp.bfloat16)
    pre_up = (hidden_grad * gate_pre * logistic).astype(jnp.bfloat16)
    input_grad = jnp.dot(pre_gate, gate_mat.T, preferred_element_type=jnp.float32)
    input_grad = (input_grad + jnp.dot(pre_up, up_mat.T, preferred_element_type=jnp.float32)).astype(jnp.bfloat16)
    return expert_out, input_grad


def reference(tokens, routes, route_gates, w_gate, w_up, w_down, cotangent):
    n_tok = tokens.shape[0]
    blocks = n_tok // TOK_DEV
    n_pair = n_tok * TOPK
    per_block = routes.reshape(blocks, TOK_DEV * TOPK)
    onehot = (per_block[:, :, None] == jnp.arange(EXPERTS, dtype=jnp.int32)[None, None, :]).astype(jnp.int32)
    slot_rank = jnp.sum((jnp.cumsum(onehot, axis=1) - onehot) * onehot, axis=2)
    slot_place = (jnp.arange(blocks, dtype=jnp.int32)[:, None] * CAP + slot_rank).reshape(-1).astype(jnp.int32)
    pair_expert = routes.reshape(-1)
    pair_ids = jnp.arange(n_pair, dtype=jnp.int32)
    pair_token = jnp.concatenate([pair_ids // TOPK, jnp.array([n_tok], jnp.int32)])
    tokens_ext = jnp.concatenate([tokens, jnp.zeros((1, D), tokens.dtype)], axis=0)
    cot_ext = jnp.concatenate([cotangent, jnp.zeros((1, D), cotangent.dtype)], axis=0)
    gates_ext = jnp.concatenate([route_gates.reshape(-1), jnp.zeros((1,), route_gates.dtype)])
    slots_all = blocks * CAP

    def one_expert(carry, inputs):
        layer_sum, grad_sum, gate_sum = carry
        expert_id, gate_mat, up_mat, down_mat = inputs
        target = jnp.where(pair_expert == expert_id, slot_place, slots_all).astype(jnp.int32)
        index = jnp.full((slots_all,), n_pair, jnp.int32).at[target].set(pair_ids, mode="drop")
        tok_index = pair_token[index]
        gate_rows = gates_ext[index]
        expert_out, input_grad = expert_pass(tokens_ext[tok_index], cot_ext[tok_index], gate_rows, gate_mat, up_mat, down_mat)
        out_float = expert_out.astype(jnp.float32)
        layer_sum = layer_sum.at[tok_index].add(gate_rows[:, None] * out_float)
        grad_sum = grad_sum.at[tok_index].add(input_grad.astype(jnp.float32))
        dots = jnp.sum(cot_ext[tok_index].astype(jnp.float32) * out_float, axis=1)
        gate_sum = gate_sum.at[index].set(dots)
        return (layer_sum, grad_sum, gate_sum), None

    start = (jnp.zeros((n_tok + 1, D), jnp.float32), jnp.zeros((n_tok + 1, D), jnp.float32), jnp.zeros((n_pair + 1,), jnp.float32))
    (layer_sum, grad_sum, gate_sum), _ = lax.scan(one_expert, start, (jnp.arange(EXPERTS, dtype=jnp.int32), w_gate, w_up, w_down))
    layer_out = layer_sum[:n_tok].astype(jnp.bfloat16)
    token_grad = grad_sum[:n_tok].astype(jnp.bfloat16)
    gate_grad = gate_sum[:n_pair].reshape(n_tok, TOPK)
    return layer_out, token_grad, gate_grad
```

```python
import functools

import jax
import jax.numpy as jnp
from jax import lax
from jax.experimental import pallas as pl
from jax.experimental.pallas import tpu as pltpu
from jax.sharding import PartitionSpec as P

BF = jnp.bfloat16
F32 = jnp.float32
NN = (((1,), (0,)), ((), ()))
NT = (((1,), (1,)), ((), ()))


def dot(a, b, dims=NN):
    return lax.dot_general(a, b, dims, preferred_element_type=F32)


def moe_kernel(
    E,
    MAIN,
    REM,
    tok_ref, cot_ref, routes_ref, gates_ref, routes_t_ref, gates_t_ref,
    wg_ref, wu_ref, wd_ref,
    lo_ref, tg_ref, gg_ref,
    wg, wu, wd,
    tok_out, grd_out, tok_in, grd_in,
    res_out, res_in, ig_out, ig_in,
    xs, gs, s_main, s_ext, p_main, p_ext,
    gate_pre, up_pre, hid_grad, hidden, pre_gate, pre_up,
    loc_sem, ws_sem, wr_sem,
    ts_sem, tr_sem, gs_sem, gr_sem,
    os_sem, or_sem, is_sem, ir_sem,
):
    T = tok_ref.shape[0]
    NB = 4
    CB = tok_ref.shape[1] // NB
    FOLD = 16 // REM
    XROW = NB * MAIN
    EXT = E * 16
    UNF = E * REM
    ROWS = E * MAIN
    dp = lax.axis_index("dp")
    me = lax.axis_index("expert")
    xp = dp + 1 - 2 * lax.rem(dp, 2)
    yp = lax.rem(dp + 2, 4)
    dg = 3 - dp

    barrier = pltpu.get_barrier_semaphore()
    for o in range(1, 4):
        pl.semaphore_signal(barrier, inc=1, device_id={"dp": lax.rem(dp + o, 4)}, device_id_type=pl.DeviceIdType.MESH)
    for o in range(1, E):
        pl.semaphore_signal(barrier, inc=1, device_id={"expert": lax.rem(me + o, E)}, device_id_type=pl.DeviceIdType.MESH)
    pl.semaphore_wait(barrier, 3 + E - 1)

    mats = ((wg_ref, wg), (wu_ref, wu), (wd_ref, wd))

    def remote(src, dst, s, r, axis, to):
        return pltpu.make_async_remote_copy(
            src_ref=src, dst_ref=dst, send_sem=s, recv_sem=r, device_id={axis: to}, device_id_type=pl.DeviceIdType.MESH
        )

    def own(m, j):
        src, buf = mats[m]
        return remote(src.at[0], buf.at[dp], ws_sem.at[m, j], wr_sem.at[m, j], "dp", (xp, yp)[j])

    def own_arrived(m, j):
        src, buf = mats[m]
        b = (xp, yp)[j]
        return remote(src.at[0], buf.at[b], ws_sem.at[m, j], wr_sem.at[m, j], "dp", b)

    def relay(m, j):
        buf = mats[m][1]
        half = buf.shape[1] // 2
        b, to = ((xp, yp), (yp, xp))[j]
        part = buf.at[b, pl.ds(j * half, half)]
        return remote(part, part, ws_sem.at[m, 2 + j], wr_sem.at[m, 2 + j], "dp", to)

    def relay_arrived(m, j):
        buf = mats[m][1]
        half = buf.shape[1] // 2
        part = buf.at[dg, pl.ds(j * half, half)]
        return remote(part, part, ws_sem.at[m, 2 + j], wr_sem.at[m, 2 + j], "dp", (yp, xp)[j])

    for m in range(2):
        for j in range(2):
            own(m, j).start()
    locs = [pltpu.make_async_copy(src.at[0], buf.at[dp], loc_sem.at[m]) for m, (src, buf) in enumerate(mats)]
    for c in locs:
        c.start()

    r_t = routes_t_ref[...]
    g_t = gates_t_ref[...]
    row_e = lax.broadcasted_iota(jnp.int32, (E, T), 0)
    hit0 = r_t[0:1, :] == row_e
    hit1 = r_t[1:2, :] == row_e
    hit = jnp.logical_or(hit0, hit1)
    before = lax.broadcasted_iota(jnp.int32, (T, T), 0) < lax.broadcasted_iota(jnp.int32, (T, T), 1)
    rank_t = dot(jnp.where(hit, 1.0, 0.0).astype(BF), jnp.where(before, 1.0, 0.0).astype(BF)).astype(jnp.int32)
    rank_t = jnp.where(hit, rank_t, -1)
    gate_t = jnp.where(hit0, g_t[0:1, :], 0.0) + jnp.where(hit1, g_t[1:2, :], 0.0)
    gsel, gsel_x = [], []
    row_m = lax.broadcasted_iota(jnp.int32, (MAIN, T), 0)
    row_x = lax.broadcasted_iota(jnp.int32, (16, T), 0)
    for e in range(E):
        rank_e = rank_t[e : e + 1, :]
        gate_e = gate_t[e : e + 1, :]
        sel = row_m == rank_e
        s_main[pl.ds(e * MAIN, MAIN), :] = jnp.where(sel, 1.0, 0.0).astype(BF)
        gsel.append(jnp.sum(jnp.where(sel, gate_e, 0.0), axis=1, keepdims=True))
        total = jnp.zeros((16, 1), F32)
        for q in range(FOLD):
            sel = jnp.logical_and(
                row_x - q * REM + MAIN == rank_e,
                jnp.logical_and(rank_e >= MAIN, jnp.logical_and(row_x >= q * REM, row_x < q * REM + REM)),
            )
            s_ext[q, pl.ds(e * 16, 16), :] = jnp.where(sel, 1.0, 0.0).astype(BF)
            total = total + jnp.sum(jnp.where(sel, gate_e, 0.0), axis=1, keepdims=True)
        gsel_x.append(total)
    gsel = jnp.concatenate(gsel, axis=0)
    gsel_x = jnp.concatenate(gsel_x, axis=0)

    def pack(src_ref, box, scale, scale_x):
        ext = jnp.zeros((EXT, CB), F32)
        for b in range(NB):
            block = src_ref[:, b * CB : (b + 1) * CB]
            rows = dot(s_main[...], block)
            if scale is not None:
                rows = rows * scale
            box[:, pl.ds(b * MAIN, MAIN), :] = rows.astype(BF).reshape(E, MAIN, CB)
            ext = ext + dot(s_ext[b], block)
        if scale is not None:
            ext = ext * scale_x
        box[:, pl.ds(XROW, 16), :] = ext.astype(BF).reshape(E, 16, CB)

    def exchange(src, dst, s, r, o):
        to = lax.rem(me + o, E)
        return remote(src.at[to], dst.at[me], s.at[o], r.at[o], "expert", to)

    def arrived(src, dst, s, r, o):
        frm = lax.rem(me + E - o, E)
        return remote(src.at[frm], dst.at[frm], s.at[o], r.at[o], "expert", frm)

    pack(tok_ref, tok_out, None, None)
    for o in range(1, E):
        exchange(tok_out, tok_in, ts_sem, tr_sem, o).start()
    tok_in[pl.ds(me, 1)] = tok_out[pl.ds(me, 1)]
    pack(cot_ref, grd_out, gsel, gsel_x)
    for o in range(1, E):
        exchange(grd_out, grd_in, gs_sem, gr_sem, o).start()
    grd_in[pl.ds(me, 1)] = grd_out[pl.ds(me, 1)]

    lane_t = lax.broadcasted_iota(jnp.int32, (T, 128), 1)
    e_of = [routes_ref[:, k : k + 1] for k in range(2)]
    named = jnp.logical_or(e_of[0] == lane_t, e_of[1] == lane_t)
    after = lax.broadcasted_iota(jnp.int32, (T, T), 0) > lax.broadcasted_iota(jnp.int32, (T, T), 1)
    rank = dot(jnp.where(after, 1.0, 0.0).astype(BF), jnp.where(named, 1.0, 0.0).astype(BF))
    lane_m = lax.broadcasted_iota(jnp.int32, (T, ROWS), 1)
    lane_x = lax.broadcasted_iota(jnp.int32, (T, EXT), 1)
    for k in range(2):
        rk = jnp.sum(jnp.where(lane_t == e_of[k], rank, 0.0), axis=1, keepdims=True).astype(jnp.int32)
        place = jnp.where(rk < MAIN, e_of[k] * MAIN + rk, -1)
        p_main[k] = jnp.where(lane_m == place, 1.0, 0.0).astype(BF)
        for q in range(FOLD):
            place = jnp.where(rk >= MAIN, e_of[k] * 16 + q * REM + rk - MAIN, -1)
            p_ext[k, q] = jnp.where(lane_x == place, 1.0, 0.0).astype(BF)

    for m in range(2):
        for j in range(2):
            own_arrived(m, j).wait_recv()
            relay(m, j).start()

    u_row = lax.broadcasted_iota(jnp.int32, (UNF, EXT), 0)
    u_col = lax.broadcasted_iota(jnp.int32, (UNF, EXT), 1)
    f_row = lax.broadcasted_iota(jnp.int32, (EXT, UNF), 0)
    f_col = lax.broadcasted_iota(jnp.int32, (EXT, UNF), 1)

    def unfold(q):
        same = (u_row // REM) * 16 + lax.rem(u_row, REM) + q * REM == u_col
        return jnp.where(same, 1.0, 0.0).astype(BF)

    def fold(q):
        same = (f_col // REM) * 16 + lax.rem(f_col, REM) + q * REM == f_row
        return jnp.where(same, 1.0, 0.0).astype(BF)

    def unpack(box, dst):
        ext = box[:, pl.ds(XROW, 16), :].reshape(EXT, CB)
        for b in range(NB):
            dst[b, pl.ds(0, ROWS), :] = box[:, pl.ds(b * MAIN, MAIN), :].reshape(ROWS, CB)
            dst[b, pl.ds(ROWS, UNF), :] = dot(unfold(b), ext).astype(BF)

    for o in range(1, E):
        arrived(tok_out, tok_in, ts_sem, tr_sem, o).wait_recv()
    unpack(tok_in, xs)
    locs[0].wait()
    locs[1].wait()
    for j in range(2):
        relay_arrived(0, j).wait_recv()
    own(2, 0).start()
    own(2, 1).start()

    def add_gate(b, c):
        gate_pre[...] += dot(xs[b], wg[b])
        return c

    def add_up(b, c):
        up_pre[...] += dot(xs[b], wu[b])
        return c

    gate_pre[...] = jnp.zeros_like(gate_pre)
    up_pre[...] = jnp.zeros_like(up_pre)
    lax.fori_loop(0, NB, add_gate, 0)
    for j in range(2):
        relay_arrived(1, j).wait_recv()
    lax.fori_loop(0, NB, add_up, 0)
    gp = gate_pre[...]
    hidden[...] = (gp * jax.nn.sigmoid(gp) * up_pre[...]).astype(BF)

    def back(src, dst, s, r, i, o, start, size, to, at):
        part = pl.ds(start, size)
        return remote(src.at[to, part], dst.at[at, part], s.at[i, o], r.at[i, o], "expert", to)

    ext_sum = [jnp.zeros((EXT, CB), F32)]

    def result(i, b):
        out = dot(hidden[...], wd[b]).astype(BF)
        start = pl.multiple_of(b * MAIN, MAIN)
        res_out[:, pl.ds(start, MAIN), :] = out[:ROWS].reshape(E, MAIN, CB)
        for o in range(1, E):
            back(res_out, res_in, os_sem, or_sem, i, o, start, MAIN, lax.rem(me + o, E), me).start()
        ext_sum[0] = ext_sum[0] + dot(fold(b), out[ROWS:])

    locs[2].wait()
    result(0, dp)
    for o in range(1, E):
        arrived(grd_out, grd_in, gs_sem, gr_sem, o).wait_recv()
    unpack(grd_in, gs)
    for j in range(2):
        own_arrived(2, j).wait_recv()
        relay(2, j).start()
    result(1, xp)
    result(2, yp)

    def add_grad(b):
        hid_grad[...] += dot(gs[b], wd[b], NT)

    hid_grad[...] = jnp.zeros_like(hid_grad)
    for b in (dp, xp, yp):
        add_grad(b)
    for j in range(2):
        relay_arrived(2, j).wait_recv()
    result(3, dg)
    res_out[:, pl.ds(XROW, 16), :] = ext_sum[0].astype(BF).reshape(E, 16, CB)
    for o in range(1, E):
        back(res_out, res_in, os_sem, or_sem, 4, o, XROW, 16, lax.rem(me + o, E), me).start()
    res_in[pl.ds(me, 1)] = res_out[pl.ds(me, 1)]
    add_grad(dg)

    gp = gate_pre[...]
    up = up_pre[...]
    hg = hid_grad[...]
    sg = jax.nn.sigmoid(gp)
    pre_gate[...] = (hg * up * sg * (1.0 + gp * (1.0 - sg))).astype(BF)
    pre_up[...] = (hg * gp * sg).astype(BF)
    ext = jnp.zeros((EXT, CB), F32)
    for b in range(NB):
        grad = (dot(pre_gate[...], wg[b], NT) + dot(pre_up[...], wu[b], NT)).astype(BF)
        ig_out[:, pl.ds(b * MAIN, MAIN), :] = grad[:ROWS].reshape(E, MAIN, CB)
        ext = ext + dot(fold(b), grad[ROWS:])
        size = MAIN
        if b == NB - 1:
            ig_out[:, pl.ds(XROW, 16), :] = ext.astype(BF).reshape(E, 16, CB)
            size = MAIN + 16
        for o in range(1, E):
            back(ig_out, ig_in, is_sem, ir_sem, b, o, b * MAIN, size, lax.rem(me + o, E), me).start()
    ig_in[pl.ds(me, 1)] = ig_out[pl.ds(me, 1)]

    for i, b in enumerate((dp, xp, yp, dg)):
        for o in range(1, E):
            frm = lax.rem(me + E - o, E)
            back(res_out, res_in, os_sem, or_sem, i, o, pl.multiple_of(b * MAIN, MAIN), MAIN, frm, frm).wait_recv()
    for o in range(1, E):
        frm = lax.rem(me + E - o, E)
        back(res_out, res_in, os_sem, or_sem, 4, o, XROW, 16, frm, frm).wait_recv()

    def pairs(box, b, ext):
        rows = box[:, pl.ds(b * MAIN, MAIN), :].reshape(ROWS, CB)
        return [dot(p_main[k], rows) + dot(p_ext[k, b], ext) for k in range(2)]

    ext = res_in[:, pl.ds(XROW, 16), :].reshape(EXT, CB)
    dots = [jnp.zeros((T, 1), F32) for _ in range(2)]
    for b in range(NB):
        cols = slice(b * CB, (b + 1) * CB)
        two = pairs(res_in, b, ext)
        cot = cot_ref[:, cols].astype(F32)
        lo_ref[:, cols] = (gates_ref[:, 0:1] * two[0] + gates_ref[:, 1:2] * two[1]).astype(BF)
        dots = [dots[k] + jnp.sum(cot * two[k], axis=1, keepdims=True) for k in range(2)]
    gg_ref[...] = jnp.concatenate(dots, axis=1)

    for b in range(NB):
        size = MAIN + 16 if b == NB - 1 else MAIN
        for o in range(1, E):
            frm = lax.rem(me + E - o, E)
            back(ig_out, ig_in, is_sem, ir_sem, b, o, b * MAIN, size, frm, frm).wait_recv()
    ext = ig_in[:, pl.ds(XROW, 16), :].reshape(EXT, CB)
    for b in range(NB):
        two = pairs(ig_in, b, ext)
        tg_ref[:, b * CB : (b + 1) * CB] = (two[0] + two[1]).astype(BF)

    for m in range(3):
        for j in range(2):
            own(m, j).wait_send()
            relay(m, j).wait_send()
    for o in range(1, E):
        exchange(tok_out, tok_in, ts_sem, tr_sem, o).wait_send()
        exchange(grd_out, grd_in, gs_sem, gr_sem, o).wait_send()
        to = lax.rem(me + o, E)
        for i, b in enumerate((dp, xp, yp, dg)):
            back(res_out, res_in, os_sem, or_sem, i, o, pl.multiple_of(b * MAIN, MAIN), MAIN, to, me).wait_send()
        back(res_out, res_in, os_sem, or_sem, 4, o, XROW, 16, to, me).wait_send()
        for b in range(NB):
            size = MAIN + 16 if b == NB - 1 else MAIN
            back(ig_out, ig_in, is_sem, ir_sem, b, o, b * MAIN, size, to, me).wait_send()


def fused(MAIN, REM, tokens, routes, route_gates, w_gate, w_up, w_down, cotangent):
    E = lax.axis_size("expert")
    T, D = tokens.shape
    CB = D // 4
    FF = w_gate.shape[2]
    BOX = 4 * MAIN + 16
    R = E * (MAIN + REM)
    box = pltpu.VMEM((E, BOX, CB), BF)
    vm = pl.BlockSpec(memory_space=pltpu.VMEM)
    hb = pl.BlockSpec(memory_space=pl.ANY)
    dma = pltpu.SemaphoreType.DMA
    return pl.pallas_call(
        functools.partial(moe_kernel, E, MAIN, REM),
        out_shape=(
            jax.ShapeDtypeStruct((T, D), BF),
            jax.ShapeDtypeStruct((T, D), BF),
            jax.ShapeDtypeStruct((T, 2), F32),
        ),
        in_specs=[vm] * 6 + [hb] * 3,
        out_specs=(vm, vm, vm),
        scratch_shapes=[
            pltpu.VMEM((4, CB, FF), BF), pltpu.VMEM((4, CB, FF), BF), pltpu.VMEM((4, FF, CB), BF),
            box, box, box, box,
            box, box, box, box,
            pltpu.VMEM((4, R, CB), BF), pltpu.VMEM((4, R, CB), BF),
            pltpu.VMEM((E * MAIN, T), BF), pltpu.VMEM((16 // REM, E * 16, T), BF),
            pltpu.VMEM((2, T, E * MAIN), BF), pltpu.VMEM((2, 16 // REM, T, E * 16), BF),
            pltpu.VMEM((R, FF), F32), pltpu.VMEM((R, FF), F32), pltpu.VMEM((R, FF), F32),
            pltpu.VMEM((R, FF), BF), pltpu.VMEM((R, FF), BF), pltpu.VMEM((R, FF), BF),
            dma((3,)), dma((3, 4)), dma((3, 4)),
            dma((E,)), dma((E,)), dma((E,)), dma((E,)),
            dma((5, E)), dma((5, E)), dma((4, E)), dma((4, E)),
        ],
        compiler_params=pltpu.CompilerParams(
            collective_id=0, has_side_effects=True, vmem_limit_bytes=56 * 1024 * 1024
        ),
    )(tokens, cotangent, routes, route_gates, routes.T, route_gates.T, w_gate, w_up, w_down)


def gather(x, axis):
    n = lax.axis_size("dp")
    me = lax.axis_index("dp")
    width = x.shape[axis]
    shape = list(x.shape)
    shape[axis] = n * width
    full = lax.dynamic_update_slice_in_dim(jnp.zeros(shape, x.dtype), x, me * width, axis)
    part = x
    for step in range(1, n):
        part = lax.ppermute(part, "dp", [(i, (i + 1) % n) for i in range(n)])
        full = lax.dynamic_update_slice_in_dim(full, part, lax.rem(me - step + n, n) * width, axis)
    return full


def general(capacity, tokens, routes, route_gates, w_gate, w_up, w_down, cotangent):
    groups = lax.axis_size("expert")
    tok_rows, width = tokens.shape
    top_count = routes.shape[1]
    pair_expert = routes.reshape(-1)
    pair_token = jnp.arange(tok_rows * top_count, dtype=jnp.int32) // top_count
    onehot = (pair_expert[:, None] == jnp.arange(groups, dtype=jnp.int32)[None, :]).astype(F32)
    before = (pair_token.size, pair_token.size)
    before = lax.broadcasted_iota(jnp.int32, before, 0) > lax.broadcasted_iota(jnp.int32, before, 1)
    slot_rank = jnp.sum(dot(before.astype(F32), onehot) * onehot, axis=1).astype(jnp.int32)
    slot_place = pair_expert * capacity + slot_rank
    pair_gate = route_gates.reshape(-1)
    cot_pairs = cotangent[pair_token].astype(F32)
    row_grad = (pair_gate[:, None] * cot_pairs).astype(BF)

    def send(rows):
        box = jnp.zeros((groups * capacity, width), BF).at[slot_place].set(rows)
        return swap(box.reshape(groups, capacity, width)).reshape(groups * capacity, width)

    def swap(box):
        return lax.all_to_all(box, "expert", split_axis=0, concat_axis=0, tiled=True)

    def fetch(rows):
        back = swap(rows.astype(BF).reshape(groups, capacity, width))
        return back.reshape(groups * capacity, width)[slot_place].astype(F32)

    gate_full, up_full, down_full = gather(w_gate[0], 0), gather(w_up[0], 0), gather(w_down[0], 1)
    x = send(tokens[pair_token])
    gate_pre, up_pre = dot(x, gate_full), dot(x, up_full)
    sg = jax.nn.sigmoid(gate_pre)
    pair_out = fetch(dot((gate_pre * sg * up_pre).astype(BF), down_full))
    hid_grad = dot(send(row_grad), down_full, NT)
    pre_gate = (hid_grad * up_pre * sg * (1.0 + gate_pre * (1.0 - sg))).astype(BF)
    pre_up = (hid_grad * gate_pre * sg).astype(BF)
    pair_grad = fetch(dot(pre_gate, gate_full, NT) + dot(pre_up, up_full, NT))
    layer_out = jnp.sum((pair_gate[:, None] * pair_out).reshape(tok_rows, top_count, width), axis=1).astype(BF)
    gate_grad = jnp.sum(cot_pairs * pair_out, axis=1).reshape(tok_rows, top_count)
    token_grad = jnp.sum(pair_grad.reshape(tok_rows, top_count, width), axis=1).astype(BF)
    return (layer_out, token_grad, gate_grad)


def local(tokens, routes, route_gates, w_gate, w_up, w_down, cotangent):
    groups = lax.axis_size("expert")
    args = (tokens, routes, route_gates, w_gate, w_up, w_down, cotangent)
    capacity = 9 * tokens.shape[0] * routes.shape[1] // (8 * groups)
    main = capacity // 16 * 16
    rem = capacity - main
    if lax.axis_size("dp") == 4 and main and rem == 4 and tokens.shape[1] % 512 == 0 and groups * main <= 512:
        return fused(main, rem, *args)
    return general(capacity, *args)


def solution(mesh):
    rows = P(("dp", "expert"), None)
    in_specs = (rows, rows, rows, P("expert", "dp", None), P("expert", "dp", None), P("expert", None, "dp"), rows)
    return jax.shard_map(local, mesh=mesh, in_specs=in_specs, out_specs=(rows, rows, rows), check_vma=False)
```

```python
import functools

import jax
import jax.numpy as jnp
from jax import lax
from jax.experimental import pallas as pl
from jax.experimental.pallas import tpu as pltpu
from jax.sharding import PartitionSpec as P

BF = jnp.bfloat16
F32 = jnp.float32
NN = (((1,), (0,)), ((), ()))
NT = (((1,), (1,)), ((), ()))


def dot(a, b, dims=NN):
    return lax.dot_general(a, b, dims, preferred_element_type=F32)


def moe_kernel(
    E,
    MAIN,
    REM,
    tok_ref, cot_ref, routes_t_ref, gates_t_ref,
    wg_ref, wu_ref, wd_ref,
    lo_ref, tg_ref, gg_ref,
    wg, wu, wd,
    tok_out, grd_out, tok_in, grd_in,
    res_out, res_in, ig_out, ig_in,
    xs, gs, s_main, s_ext, p_main, p_ext,
    gate_pre, up_pre, hid_grad, hidden, pre_gate, pre_up, ext_sum, ig_sum,
    loc_sem, ws_sem, wr_sem, ds_sem, dr_sem,
    ts_sem, tr_sem, gs_sem, gr_sem,
    os_sem, or_sem, is_sem, ir_sem,
):
    T = tok_ref.shape[0]
    NB = 4
    CB = tok_ref.shape[1] // NB
    FOLD = 16 // REM
    XROW = NB * MAIN
    EXT = E * 16
    UNF = E * REM
    ROWS = E * MAIN
    dp = lax.axis_index("dp")
    me = lax.axis_index("expert")
    xp = dp + 1 - 2 * lax.rem(dp, 2)
    yp = lax.rem(dp + 2, 4)
    dg = 3 - dp

    barrier = pltpu.get_barrier_semaphore()
    for o in range(1, 4):
        pl.semaphore_signal(barrier, inc=1, device_id={"dp": lax.rem(dp + o, 4)}, device_id_type=pl.DeviceIdType.MESH)
    for o in range(1, E):
        pl.semaphore_signal(barrier, inc=1, device_id={"expert": lax.rem(me + o, E)}, device_id_type=pl.DeviceIdType.MESH)
    pl.semaphore_wait(barrier, 3 + E - 1)

    mats = ((wg_ref, wg), (wu_ref, wu), (wd_ref, wd))

    def remote(src, dst, s, r, axis, to):
        return pltpu.make_async_remote_copy(
            src_ref=src, dst_ref=dst, send_sem=s, recv_sem=r, device_id={axis: to}, device_id_type=pl.DeviceIdType.MESH
        )

    def own(m, j):
        src, buf = mats[m]
        return remote(src.at[0], buf.at[dp], ws_sem.at[m, j], wr_sem.at[m, j], "dp", (xp, yp)[j])

    def own_arrived(m, j):
        src, buf = mats[m]
        b = (xp, yp)[j]
        return remote(src.at[0], buf.at[b], ws_sem.at[m, j], wr_sem.at[m, j], "dp", b)

    CUT = (CB + 255) // 256 * 128
    parts = ((0, CUT), (CUT, CB - CUT))

    def down(j, h):
        cols = pl.ds(*parts[h])
        return remote(wd_ref.at[0, :, cols], wd.at[dp, :, cols], ds_sem.at[j, h], dr_sem.at[j, h], "dp", (xp, yp)[j])

    def down_arrived(j, h):
        cols = pl.ds(*parts[h])
        b = (xp, yp)[j]
        return remote(wd_ref.at[0, :, cols], wd.at[b, :, cols], ds_sem.at[j, h], dr_sem.at[j, h], "dp", b)

    def relay(m, j):
        buf = mats[m][1]
        half = buf.shape[1] // 2
        b, to = ((xp, yp), (yp, xp))[j]
        part = buf.at[b, pl.ds(j * half, half)]
        return remote(part, part, ws_sem.at[m, 2 + j], wr_sem.at[m, 2 + j], "dp", to)

    def relay_arrived(m, j):
        buf = mats[m][1]
        half = buf.shape[1] // 2
        part = buf.at[dg, pl.ds(j * half, half)]
        return remote(part, part, ws_sem.at[m, 2 + j], wr_sem.at[m, 2 + j], "dp", (yp, xp)[j])

    for m in range(2):
        for j in range(2):
            own(m, j).start()
    locs = [pltpu.make_async_copy(src.at[0], buf.at[dp], loc_sem.at[m]) for m, (src, buf) in enumerate(mats)]
    for c in locs:
        c.start()

    r_t = routes_t_ref[...]
    g_t = gates_t_ref[...]
    row_e = lax.broadcasted_iota(jnp.int32, (E, T), 0)
    hit0 = r_t[0:1, :] == row_e
    hit1 = r_t[1:2, :] == row_e
    hit = jnp.logical_or(hit0, hit1)
    before = lax.broadcasted_iota(jnp.int32, (T, T), 0) < lax.broadcasted_iota(jnp.int32, (T, T), 1)
    rank_t = dot(jnp.where(hit, 1.0, 0.0).astype(BF), jnp.where(before, 1.0, 0.0).astype(BF)).astype(jnp.int32)
    rank_t = jnp.where(hit, rank_t, -1)
    gate_t = jnp.where(hit0, g_t[0:1, :], 0.0) + jnp.where(hit1, g_t[1:2, :], 0.0)
    row_m = lax.broadcasted_iota(jnp.int32, (MAIN, T), 0)
    row_x = lax.broadcasted_iota(jnp.int32, (16, T), 0)
    for e in range(E):
        rank_e = rank_t[e : e + 1, :]
        s_main[pl.ds(e * MAIN, MAIN), :] = jnp.where(row_m == rank_e, 1.0, 0.0).astype(BF)
        for q in range(FOLD):
            sel = jnp.logical_and(
                row_x - q * REM + MAIN == rank_e,
                jnp.logical_and(rank_e >= MAIN, jnp.logical_and(row_x >= q * REM, row_x < q * REM + REM)),
            )
            s_ext[q, pl.ds(e * 16, 16), :] = jnp.where(sel, 1.0, 0.0).astype(BF)

    def pack(src_ref, box, scale, scale_x):
        ext = jnp.zeros((EXT, CB), F32)
        for b in range(NB):
            block = src_ref[:, b * CB : (b + 1) * CB]
            rows = dot(s_main[...], block)
            if scale is not None:
                rows = rows * scale
            box[:, pl.ds(b * MAIN, MAIN), :] = rows.astype(BF).reshape(E, MAIN, CB)
            ext = ext + dot(s_ext[b], block)
        if scale is not None:
            ext = ext * scale_x
        box[:, pl.ds(XROW, 16), :] = ext.astype(BF).reshape(E, 16, CB)

    def exchange(src, dst, s, r, o):
        to = lax.rem(me + o, E)
        return remote(src.at[to], dst.at[me], s.at[o], r.at[o], "expert", to)

    def arrived(src, dst, s, r, o):
        frm = lax.rem(me + E - o, E)
        return remote(src.at[frm], dst.at[frm], s.at[o], r.at[o], "expert", frm)

    pack(tok_ref, tok_out, None, None)
    for o in range(1, E):
        exchange(tok_out, tok_in, ts_sem, tr_sem, o).start()
    tok_in[pl.ds(me, 1)] = tok_out[pl.ds(me, 1)]
    gsel, gsel_x = [], []
    for e in range(E):
        gate_e = gate_t[e : e + 1, :]
        sel = s_main[pl.ds(e * MAIN, MAIN), :].astype(F32)
        gsel.append(jnp.sum(sel * gate_e, axis=1, keepdims=True))
        sel = sum(s_ext[q, pl.ds(e * 16, 16), :].astype(F32) for q in range(FOLD))
        gsel_x.append(jnp.sum(sel * gate_e, axis=1, keepdims=True))
    pack(cot_ref, grd_out, jnp.concatenate(gsel, axis=0), jnp.concatenate(gsel_x, axis=0))
    for o in range(1, E):
        exchange(grd_out, grd_in, gs_sem, gr_sem, o).start()
    grd_in[pl.ds(me, 1)] = grd_out[pl.ds(me, 1)]

    ranks = rank_t.astype(F32)
    turned = [r_t[k : k + 1, :].astype(F32) for k in range(2)]
    turned += [jnp.sum(jnp.where(h, ranks, 0.0), axis=0, keepdims=True) for h in (hit0, hit1)]
    turned += [g_t[0:1, :], g_t[1:2, :], jnp.zeros((2, T), F32)]
    turned = jnp.concatenate(turned, axis=0).T
    gates = [turned[:, 4 + k : 5 + k] for k in range(2)]
    lane_m = lax.broadcasted_iota(jnp.int32, (T, ROWS), 1)
    lane_x = lax.broadcasted_iota(jnp.int32, (T, EXT), 1)
    for k in range(2):
        e_k = turned[:, k : k + 1].astype(jnp.int32)
        rk = turned[:, 2 + k : 3 + k].astype(jnp.int32)
        place = jnp.where(rk < MAIN, e_k * MAIN + rk, -1)
        p_main[k] = jnp.where(lane_m == place, 1.0, 0.0).astype(BF)
        for q in range(FOLD):
            place = jnp.where(rk >= MAIN, e_k * 16 + q * REM + rk - MAIN, -1)
            p_ext[k, q] = jnp.where(lane_x == place, 1.0, 0.0).astype(BF)

    for m in range(2):
        for j in range(2):
            own_arrived(m, j).wait_recv()
            relay(m, j).start()

    u_row = lax.broadcasted_iota(jnp.int32, (UNF, EXT), 0)
    u_col = lax.broadcasted_iota(jnp.int32, (UNF, EXT), 1)
    f_row = lax.broadcasted_iota(jnp.int32, (EXT, UNF), 0)
    f_col = lax.broadcasted_iota(jnp.int32, (EXT, UNF), 1)

    def unfold(q):
        same = (u_row // REM) * 16 + lax.rem(u_row, REM) + q * REM == u_col
        return jnp.where(same, 1.0, 0.0).astype(BF)

    def fold(q):
        same = (f_col // REM) * 16 + lax.rem(f_col, REM) + q * REM == f_row
        return jnp.where(same, 1.0, 0.0).astype(BF)

    def unpack(box, dst):
        ext = box[:, pl.ds(XROW, 16), :].reshape(EXT, CB)
        for b in range(NB):
            dst[b, pl.ds(0, ROWS), :] = box[:, pl.ds(b * MAIN, MAIN), :].reshape(ROWS, CB)
            dst[b, pl.ds(ROWS, UNF), :] = dot(unfold(b), ext).astype(BF)

    for j in range(2):
        relay_arrived(0, j).wait_recv()
    for h in range(2):
        for j in range(2):
            down(j, h).start()
    for o in range(1, E):
        arrived(tok_out, tok_in, ts_sem, tr_sem, o).wait_recv()
    unpack(tok_in, xs)
    locs[0].wait()
    locs[1].wait()

    def add_gate(b):
        gate_pre[...] += dot(xs[b], wg[b])

    def add_up(b):
        up_pre[...] += dot(xs[b], wu[b])

    gate_pre[...] = dot(xs[dp], wg[dp])
    up_pre[...] = dot(xs[dp], wu[dp])
    for b in (xp, yp):
        add_gate(b)
        add_up(b)
    add_gate(dg)
    for j in range(2):
        relay_arrived(1, j).wait_recv()
    add_up(dg)
    gp = gate_pre[...]
    hidden[...] = (gp * jax.nn.sigmoid(gp) * up_pre[...]).astype(BF)

    def back(src, dst, s, r, i, o, start, size, to, at):
        part = pl.ds(start, size)
        return remote(src.at[to, part], dst.at[at, part], s.at[i, o], r.at[i, o], "expert", to)

    steps = [(dp, 0, CB)] + [(b, *part) for part in parts for b in (xp, yp)] + [(dg, 0, CB)]
    LAST = len(steps)

    def back_out(i, o, to, at):
        b, first, width = steps[i]
        part = (pl.ds(pl.multiple_of(b * MAIN, MAIN), MAIN), pl.ds(first, width))
        return remote(
            res_out.at[(to, *part)], res_in.at[(at, *part)], os_sem.at[i, o], or_sem.at[i, o], "expert", to
        )

    ext_sum[...] = jnp.zeros_like(ext_sum)

    def result(i):
        b, first, width = steps[i]
        cols = slice(first, first + width)
        out = dot(hidden[...], wd[b, :, cols]).astype(BF)
        start = pl.multiple_of(b * MAIN, MAIN)
        res_out[:, pl.ds(start, MAIN), cols] = out[:ROWS].reshape(E, MAIN, width)
        for o in range(1, E):
            back_out(i, o, lax.rem(me + o, E), me).start()
        ext_sum[:, cols] += dot(fold(b), out[ROWS:])

    locs[2].wait()
    result(0)
    for o in range(1, E):
        arrived(grd_out, grd_in, gs_sem, gr_sem, o).wait_recv()
    unpack(grd_in, gs)
    for h in range(2):
        for j in range(2):
            down_arrived(j, h).wait_recv()
            if h == 1:
                relay(2, j).start()
        result(1 + 2 * h)
        result(2 + 2 * h)

    def add_grad(b):
        hid_grad[...] += dot(gs[b], wd[b], NT)

    hid_grad[...] = jnp.zeros_like(hid_grad)
    for b in (dp, xp, yp):
        add_grad(b)
    for j in range(2):
        relay_arrived(2, j).wait_recv()
    result(LAST - 1)
    res_out[:, pl.ds(XROW, 16), :] = ext_sum[...].astype(BF).reshape(E, 16, CB)
    for o in range(1, E):
        back(res_out, res_in, os_sem, or_sem, LAST, o, XROW, 16, lax.rem(me + o, E), me).start()
    res_in[pl.ds(me, 1)] = res_out[pl.ds(me, 1)]
    add_grad(dg)

    gp = gate_pre[...]
    up = up_pre[...]
    hg = hid_grad[...]
    sg = jax.nn.sigmoid(gp)
    pre_gate[...] = (hg * up * sg * (1.0 + gp * (1.0 - sg))).astype(BF)
    pre_up[...] = (hg * gp * sg).astype(BF)
    ext = jnp.zeros((EXT, CB), F32)
    for b in range(NB):
        grad = (dot(pre_gate[...], wg[b], NT) + dot(pre_up[...], wu[b], NT)).astype(BF)
        ig_out[:, pl.ds(b * MAIN, MAIN), :] = grad[:ROWS].reshape(E, MAIN, CB)
        ext = ext + dot(fold(b), grad[ROWS:])
        size = MAIN
        if b == NB - 1:
            ig_out[:, pl.ds(XROW, 16), :] = ext.astype(BF).reshape(E, 16, CB)
            size = MAIN + 16
        for o in range(1, E):
            back(ig_out, ig_in, is_sem, ir_sem, b, o, b * MAIN, size, lax.rem(me + o, E), me).start()
    ig_in[pl.ds(me, 1)] = ig_out[pl.ds(me, 1)]

    for i in range(LAST):
        for o in range(1, E):
            frm = lax.rem(me + E - o, E)
            back_out(i, o, frm, frm).wait_recv()
    for o in range(1, E):
        frm = lax.rem(me + E - o, E)
        back(res_out, res_in, os_sem, or_sem, LAST, o, XROW, 16, frm, frm).wait_recv()

    def pairs(box, b, ext):
        rows = box[:, pl.ds(b * MAIN, MAIN), :].reshape(ROWS, CB)
        return [dot(p_main[k], rows) + dot(p_ext[k, b], ext) for k in range(2)]

    ext = res_in[:, pl.ds(XROW, 16), :].reshape(EXT, CB)
    dots = [jnp.zeros((T, 1), F32) for _ in range(2)]
    for b in range(NB):
        cols = slice(b * CB, (b + 1) * CB)
        two = pairs(res_in, b, ext)
        cot = cot_ref[:, cols].astype(F32)
        lo_ref[:, cols] = (gates[0] * two[0] + gates[1] * two[1]).astype(BF)
        dots = [dots[k] + jnp.sum(cot * two[k], axis=1, keepdims=True) for k in range(2)]
    lane = lax.broadcasted_iota(jnp.int32, (T, 8), 1)
    gg_ref[...] = jnp.where(lane == 0, dots[0], jnp.where(lane == 1, dots[1], 0.0)).T[0:2, :]

    both = p_main[0] + p_main[1]
    for b in range(NB):
        size = MAIN + 16 if b == NB - 1 else MAIN
        for o in range(1, E):
            frm = lax.rem(me + E - o, E)
            back(ig_out, ig_in, is_sem, ir_sem, b, o, b * MAIN, size, frm, frm).wait_recv()
        rows = ig_in[:, pl.ds(b * MAIN, MAIN), :].reshape(ROWS, CB)
        if b < NB - 1:
            ig_sum[b] = dot(both, rows)
        else:
            ext = ig_in[:, pl.ds(XROW, 16), :].reshape(EXT, CB)
            tg_ref[:, b * CB :] = (dot(both, rows) + dot(p_ext[0, b] + p_ext[1, b], ext)).astype(BF)
    for b in range(NB - 1):
        total = ig_sum[b] + dot(p_ext[0, b] + p_ext[1, b], ext)
        tg_ref[:, b * CB : (b + 1) * CB] = total.astype(BF)

    for j in range(2):
        for m in range(3):
            relay(m, j).wait_send()
        for m in range(2):
            own(m, j).wait_send()
            down(j, m).wait_send()
    for o in range(1, E):
        exchange(tok_out, tok_in, ts_sem, tr_sem, o).wait_send()
        exchange(grd_out, grd_in, gs_sem, gr_sem, o).wait_send()
        to = lax.rem(me + o, E)
        for i in range(LAST):
            back_out(i, o, to, me).wait_send()
        back(res_out, res_in, os_sem, or_sem, LAST, o, XROW, 16, to, me).wait_send()
        for b in range(NB):
            size = MAIN + 16 if b == NB - 1 else MAIN
            back(ig_out, ig_in, is_sem, ir_sem, b, o, b * MAIN, size, to, me).wait_send()


def fused(MAIN, REM, tokens, routes, route_gates, w_gate, w_up, w_down, cotangent):
    E = lax.axis_size("expert")
    T, D = tokens.shape
    CB = D // 4
    FF = w_gate.shape[2]
    BOX = 4 * MAIN + 16
    R = E * (MAIN + REM)
    box = pltpu.VMEM((E, BOX, CB), BF)
    vm = pl.BlockSpec(memory_space=pltpu.VMEM)
    hb = pl.BlockSpec(memory_space=pl.ANY)
    dma = pltpu.SemaphoreType.DMA
    layer_out, token_grad, gate_grad = pl.pallas_call(
        functools.partial(moe_kernel, E, MAIN, REM),
        out_shape=(
            jax.ShapeDtypeStruct((T, D), BF),
            jax.ShapeDtypeStruct((T, D), BF),
            jax.ShapeDtypeStruct((2, T), F32),
        ),
        in_specs=[vm] * 4 + [hb] * 3,
        out_specs=(vm, vm, vm),
        scratch_shapes=[
            pltpu.VMEM((4, CB, FF), BF), pltpu.VMEM((4, CB, FF), BF), pltpu.VMEM((4, FF, CB), BF),
            box, box, box, box,
            box, box, box, box,
            pltpu.VMEM((4, R, CB), BF), pltpu.VMEM((4, R, CB), BF),
            pltpu.VMEM((E * MAIN, T), BF), pltpu.VMEM((16 // REM, E * 16, T), BF),
            pltpu.VMEM((2, T, E * MAIN), BF), pltpu.VMEM((2, 16 // REM, T, E * 16), BF),
            pltpu.VMEM((R, FF), F32), pltpu.VMEM((R, FF), F32), pltpu.VMEM((R, FF), F32),
            pltpu.VMEM((R, FF), BF), pltpu.VMEM((R, FF), BF), pltpu.VMEM((R, FF), BF), pltpu.VMEM((E * 16, CB), F32), pltpu.VMEM((3, T, CB), F32),
            dma((3,)), dma((3, 4)), dma((3, 4)), dma((2, 2)), dma((2, 2)),
            dma((E,)), dma((E,)), dma((E,)), dma((E,)),
            dma((7, E)), dma((7, E)), dma((4, E)), dma((4, E)),
        ],
        compiler_params=pltpu.CompilerParams(
            collective_id=0, has_side_effects=True, vmem_limit_bytes=56 * 1024 * 1024
        ),
    )(tokens, cotangent, routes.T, route_gates.T, w_gate, w_up, w_down)
    return layer_out, token_grad, gate_grad.T


def gather(x, axis):
    n = lax.axis_size("dp")
    me = lax.axis_index("dp")
    width = x.shape[axis]
    shape = list(x.shape)
    shape[axis] = n * width
    full = lax.dynamic_update_slice_in_dim(jnp.zeros(shape, x.dtype), x, me * width, axis)
    part = x
    for step in range(1, n):
        part = lax.ppermute(part, "dp", [(i, (i + 1) % n) for i in range(n)])
        full = lax.dynamic_update_slice_in_dim(full, part, lax.rem(me - step + n, n) * width, axis)
    return full


def general(capacity, tokens, routes, route_gates, w_gate, w_up, w_down, cotangent):
    groups = lax.axis_size("expert")
    tok_rows, width = tokens.shape
    top_count = routes.shape[1]
    pair_expert = routes.reshape(-1)
    pair_token = jnp.arange(tok_rows * top_count, dtype=jnp.int32) // top_count
    onehot = (pair_expert[:, None] == jnp.arange(groups, dtype=jnp.int32)[None, :]).astype(F32)
    before = (pair_token.size, pair_token.size)
    before = lax.broadcasted_iota(jnp.int32, before, 0) > lax.broadcasted_iota(jnp.int32, before, 1)
    slot_rank = jnp.sum(dot(before.astype(F32), onehot) * onehot, axis=1).astype(jnp.int32)
    slot_place = pair_expert * capacity + slot_rank
    pair_gate = route_gates.reshape(-1)
    cot_pairs = cotangent[pair_token].astype(F32)
    row_grad = (pair_gate[:, None] * cot_pairs).astype(BF)

    def send(rows):
        box = jnp.zeros((groups * capacity, width), BF).at[slot_place].set(rows)
        return swap(box.reshape(groups, capacity, width)).reshape(groups * capacity, width)

    def swap(box):
        return lax.all_to_all(box, "expert", split_axis=0, concat_axis=0, tiled=True)

    def fetch(rows):
        back = swap(rows.astype(BF).reshape(groups, capacity, width))
        return back.reshape(groups * capacity, width)[slot_place].astype(F32)

    gate_full, up_full, down_full = gather(w_gate[0], 0), gather(w_up[0], 0), gather(w_down[0], 1)
    x = send(tokens[pair_token])
    gate_pre, up_pre = dot(x, gate_full), dot(x, up_full)
    sg = jax.nn.sigmoid(gate_pre)
    pair_out = fetch(dot((gate_pre * sg * up_pre).astype(BF), down_full))
    hid_grad = dot(send(row_grad), down_full, NT)
    pre_gate = (hid_grad * up_pre * sg * (1.0 + gate_pre * (1.0 - sg))).astype(BF)
    pre_up = (hid_grad * gate_pre * sg).astype(BF)
    pair_grad = fetch(dot(pre_gate, gate_full, NT) + dot(pre_up, up_full, NT))
    layer_out = jnp.sum((pair_gate[:, None] * pair_out).reshape(tok_rows, top_count, width), axis=1).astype(BF)
    gate_grad = jnp.sum(cot_pairs * pair_out, axis=1).reshape(tok_rows, top_count)
    token_grad = jnp.sum(pair_grad.reshape(tok_rows, top_count, width), axis=1).astype(BF)
    return (layer_out, token_grad, gate_grad)


def local(tokens, routes, route_gates, w_gate, w_up, w_down, cotangent):
    groups = lax.axis_size("expert")
    args = (tokens, routes, route_gates, w_gate, w_up, w_down, cotangent)
    capacity = 9 * tokens.shape[0] * routes.shape[1] // (8 * groups)
    main = capacity // 16 * 16
    rem = capacity - main
    if lax.axis_size("dp") == 4 and main and rem == 4 and tokens.shape[1] % 512 == 0 and groups * main <= 512:
        return fused(main, rem, *args)
    return general(capacity, *args)


def solution(mesh):
    rows = P(("dp", "expert"), None)
    in_specs = (rows, rows, rows, P("expert", "dp", None), P("expert", "dp", None), P("expert", None, "dp"), rows)
    return jax.shard_map(local, mesh=mesh, in_specs=in_specs, out_specs=(rows, rows, rows), check_vma=False)
```

```python
import functools

import jax
import jax.numpy as jnp
from jax import lax
from jax.experimental import pallas as pl
from jax.experimental.pallas import tpu as pltpu
from jax.sharding import PartitionSpec as P

BF = jnp.bfloat16
F32 = jnp.float32
NN = (((1,), (0,)), ((), ()))
NT = (((1,), (1,)), ((), ()))


def dot(a, b, dims=NN):
    return lax.dot_general(a, b, dims, preferred_element_type=F32)


def moe_kernel(
    E,
    MAIN,
    REM,
    tok_ref, cot_ref, routes_t_ref, gates_t_ref,
    wg_ref, wu_ref, wd_ref,
    lo_ref, tg_ref, gg_ref,
    wg, wu, wd,
    tok_out, grd_out, tok_in, grd_in,
    res_out, res_in, ig_out, ig_in,
    xs, gs, s_main, s_ext, p_main, p_ext,
    gate_pre, up_pre, hid_grad, hidden, pre_gate, pre_up, ext_sum, ig_sum,
    loc_sem, ws_sem, wr_sem, ds_sem, dr_sem,
    ts_sem, tr_sem, gs_sem, gr_sem,
    os_sem, or_sem, is_sem, ir_sem,
):
    T = tok_ref.shape[0]
    NB = 4
    CB = tok_ref.shape[1] // NB
    FOLD = 16 // REM
    XROW = NB * MAIN
    EXT = E * 16
    UNF = E * REM
    ROWS = E * MAIN
    dp = lax.axis_index("dp")
    me = lax.axis_index("expert")
    xp = dp + 1 - 2 * lax.rem(dp, 2)
    yp = lax.rem(dp + 2, 4)
    dg = 3 - dp

    barrier = pltpu.get_barrier_semaphore()
    for o in range(1, 4):
        pl.semaphore_signal(barrier, inc=1, device_id={"dp": lax.rem(dp + o, 4)}, device_id_type=pl.DeviceIdType.MESH)
    for o in range(1, E):
        pl.semaphore_signal(barrier, inc=1, device_id={"expert": lax.rem(me + o, E)}, device_id_type=pl.DeviceIdType.MESH)
    pl.semaphore_wait(barrier, 3 + E - 1)

    mats = ((wg_ref, wg), (wu_ref, wu), (wd_ref, wd))

    def remote(src, dst, s, r, axis, to):
        return pltpu.make_async_remote_copy(
            src_ref=src, dst_ref=dst, send_sem=s, recv_sem=r, device_id={axis: to}, device_id_type=pl.DeviceIdType.MESH
        )

    def own(m, j):
        src, buf = mats[m]
        return remote(src.at[0], buf.at[dp], ws_sem.at[m, j], wr_sem.at[m, j], "dp", (xp, yp)[j])

    def own_arrived(m, j):
        src, buf = mats[m]
        b = (xp, yp)[j]
        return remote(src.at[0], buf.at[b], ws_sem.at[m, j], wr_sem.at[m, j], "dp", b)

    CUT = (CB + 255) // 256 * 128
    parts = ((0, CUT), (CUT, CB - CUT))

    def down(j, h):
        cols = pl.ds(*parts[h])
        return remote(wd_ref.at[0, :, cols], wd.at[dp, :, cols], ds_sem.at[j, h], dr_sem.at[j, h], "dp", (xp, yp)[j])

    def down_arrived(j, h):
        cols = pl.ds(*parts[h])
        b = (xp, yp)[j]
        return remote(wd_ref.at[0, :, cols], wd.at[b, :, cols], ds_sem.at[j, h], dr_sem.at[j, h], "dp", b)

    def relay(m, j):
        buf = mats[m][1]
        half = buf.shape[1] // 2
        b, to = ((xp, yp), (yp, xp))[j]
        part = buf.at[b, pl.ds(j * half, half)]
        return remote(part, part, ws_sem.at[m, 2 + j], wr_sem.at[m, 2 + j], "dp", to)

    def relay_arrived(m, j):
        buf = mats[m][1]
        half = buf.shape[1] // 2
        part = buf.at[dg, pl.ds(j * half, half)]
        return remote(part, part, ws_sem.at[m, 2 + j], wr_sem.at[m, 2 + j], "dp", (yp, xp)[j])

    for m in range(2):
        for j in range(2):
            own(m, j).start()
    locs = [pltpu.make_async_copy(src.at[0], buf.at[dp], loc_sem.at[m]) for m, (src, buf) in enumerate(mats)]
    for c in locs:
        c.start()

    r_t = routes_t_ref[...]
    g_t = gates_t_ref[...]
    row_e = lax.broadcasted_iota(jnp.int32, (E, T), 0)
    hit0 = r_t[0:1, :] == row_e
    hit1 = r_t[1:2, :] == row_e
    hit = jnp.logical_or(hit0, hit1)
    before = lax.broadcasted_iota(jnp.int32, (T, T), 0) < lax.broadcasted_iota(jnp.int32, (T, T), 1)
    rank_t = dot(jnp.where(hit, 1.0, 0.0).astype(BF), jnp.where(before, 1.0, 0.0).astype(BF)).astype(jnp.int32)
    rank_t = jnp.where(hit, rank_t, -1)
    gate_t = jnp.where(hit0, g_t[0:1, :], 0.0) + jnp.where(hit1, g_t[1:2, :], 0.0)
    row_m = lax.broadcasted_iota(jnp.int32, (MAIN, T), 0)
    row_x = lax.broadcasted_iota(jnp.int32, (16, T), 0)
    for e in range(E):
        rank_e = rank_t[e : e + 1, :]
        s_main[pl.ds(e * MAIN, MAIN), :] = jnp.where(row_m == rank_e, 1.0, 0.0).astype(BF)
        for q in range(FOLD):
            sel = jnp.logical_and(
                row_x - q * REM + MAIN == rank_e,
                jnp.logical_and(rank_e >= MAIN, jnp.logical_and(row_x >= q * REM, row_x < q * REM + REM)),
            )
            s_ext[q, pl.ds(e * 16, 16), :] = jnp.where(sel, 1.0, 0.0).astype(BF)

    def pack(src_ref, box, scale, scale_x):
        ext = jnp.zeros((EXT, CB), F32)
        for b in range(NB):
            block = src_ref[:, b * CB : (b + 1) * CB]
            rows = dot(s_main[...], block)
            if scale is not None:
                rows = rows * scale
            box[:, pl.ds(b * MAIN, MAIN), :] = rows.astype(BF).reshape(E, MAIN, CB)
            ext = ext + dot(s_ext[b], block)
        if scale is not None:
            ext = ext * scale_x
        box[:, pl.ds(XROW, 16), :] = ext.astype(BF).reshape(E, 16, CB)

    def exchange(src, dst, s, r, o):
        to = lax.rem(me + o, E)
        return remote(src.at[to], dst.at[me], s.at[o], r.at[o], "expert", to)

    def arrived(src, dst, s, r, o):
        frm = lax.rem(me + E - o, E)
        return remote(src.at[frm], dst.at[frm], s.at[o], r.at[o], "expert", frm)

    pack(tok_ref, tok_out, None, None)
    for o in range(1, E):
        exchange(tok_out, tok_in, ts_sem, tr_sem, o).start()
    tok_in[pl.ds(me, 1)] = tok_out[pl.ds(me, 1)]
    gsel, gsel_x = [], []
    for e in range(E):
        gate_e = gate_t[e : e + 1, :]
        sel = s_main[pl.ds(e * MAIN, MAIN), :].astype(F32)
        gsel.append(jnp.sum(sel * gate_e, axis=1, keepdims=True))
        sel = sum(s_ext[q, pl.ds(e * 16, 16), :].astype(F32) for q in range(FOLD))
        gsel_x.append(jnp.sum(sel * gate_e, axis=1, keepdims=True))
    pack(cot_ref, grd_out, jnp.concatenate(gsel, axis=0), jnp.concatenate(gsel_x, axis=0))
    grd_in[pl.ds(me, 1)] = grd_out[pl.ds(me, 1)]

    ranks = rank_t.astype(F32)
    turned = [r_t[k : k + 1, :].astype(F32) for k in range(2)]
    turned += [jnp.sum(jnp.where(h, ranks, 0.0), axis=0, keepdims=True) for h in (hit0, hit1)]
    turned += [g_t[0:1, :], g_t[1:2, :], jnp.zeros((2, T), F32)]
    turned = jnp.concatenate(turned, axis=0).T
    gates = [turned[:, 4 + k : 5 + k] for k in range(2)]
    lane_m = lax.broadcasted_iota(jnp.int32, (T, ROWS), 1)
    lane_x = lax.broadcasted_iota(jnp.int32, (T, EXT), 1)
    for k in range(2):
        e_k = turned[:, k : k + 1].astype(jnp.int32)
        rk = turned[:, 2 + k : 3 + k].astype(jnp.int32)
        place = jnp.where(rk < MAIN, e_k * MAIN + rk, -1)
        p_main[k] = jnp.where(lane_m == place, 1.0, 0.0).astype(BF)
        for q in range(FOLD):
            place = jnp.where(rk >= MAIN, e_k * 16 + q * REM + rk - MAIN, -1)
            p_ext[k, q] = jnp.where(lane_x == place, 1.0, 0.0).astype(BF)

    u_row = lax.broadcasted_iota(jnp.int32, (UNF, EXT), 0)
    u_col = lax.broadcasted_iota(jnp.int32, (UNF, EXT), 1)
    f_row = lax.broadcasted_iota(jnp.int32, (EXT, UNF), 0)
    f_col = lax.broadcasted_iota(jnp.int32, (EXT, UNF), 1)

    def unfold(q):
        same = (u_row // REM) * 16 + lax.rem(u_row, REM) + q * REM == u_col
        return jnp.where(same, 1.0, 0.0).astype(BF)

    def fold(q):
        same = (f_col // REM) * 16 + lax.rem(f_col, REM) + q * REM == f_row
        return jnp.where(same, 1.0, 0.0).astype(BF)

    def unpack(box, dst):
        ext = box[:, pl.ds(XROW, 16), :].reshape(EXT, CB)
        for b in range(NB):
            dst[b, pl.ds(0, ROWS), :] = box[:, pl.ds(b * MAIN, MAIN), :].reshape(ROWS, CB)
            dst[b, pl.ds(ROWS, UNF), :] = dot(unfold(b), ext).astype(BF)

    for o in range(1, E):
        exchange(tok_out, tok_in, ts_sem, tr_sem, o).wait_send()
    for o in range(1, E):
        exchange(grd_out, grd_in, gs_sem, gr_sem, o).start()
    for o in range(1, E):
        arrived(tok_out, tok_in, ts_sem, tr_sem, o).wait_recv()
    unpack(tok_in, xs)
    locs[0].wait()
    locs[1].wait()

    def add_gate(b):
        gate_pre[...] += dot(xs[b], wg[b])

    def add_up(b):
        up_pre[...] += dot(xs[b], wu[b])

    gate_pre[...] = dot(xs[dp], wg[dp])
    up_pre[...] = dot(xs[dp], wu[dp])
    for m in range(2):
        for j in range(2):
            own_arrived(m, j).wait_recv()
            relay(m, j).start()
    for b in (xp, yp):
        add_gate(b)
        add_up(b)
    for j in range(2):
        relay_arrived(0, j).wait_recv()
    for h in range(2):
        for j in range(2):
            down(j, h).start()
    add_gate(dg)
    for j in range(2):
        relay_arrived(1, j).wait_recv()
    add_up(dg)
    gp = gate_pre[...]
    hidden[...] = (gp * jax.nn.sigmoid(gp) * up_pre[...]).astype(BF)

    def back(src, dst, s, r, i, o, start, size, to, at):
        part = pl.ds(start, size)
        return remote(src.at[to, part], dst.at[at, part], s.at[i, o], r.at[i, o], "expert", to)

    steps = [(dp, 0, CB)] + [(b, *part) for part in parts for b in (xp, yp)] + [(dg, 0, CB)]
    LAST = len(steps)

    def back_out(i, o, to, at):
        b, first, width = steps[i]
        part = (pl.ds(pl.multiple_of(b * MAIN, MAIN), MAIN), pl.ds(first, width))
        return remote(
            res_out.at[(to, *part)], res_in.at[(at, *part)], os_sem.at[i, o], or_sem.at[i, o], "expert", to
        )

    ext_sum[...] = jnp.zeros_like(ext_sum)

    def result(i):
        b, first, width = steps[i]
        cols = slice(first, first + width)
        out = dot(hidden[...], wd[b, :, cols]).astype(BF)
        start = pl.multiple_of(b * MAIN, MAIN)
        res_out[:, pl.ds(start, MAIN), cols] = out[:ROWS].reshape(E, MAIN, width)
        for o in range(1, E):
            back_out(i, o, lax.rem(me + o, E), me).start()
        ext_sum[:, cols] += dot(fold(b), out[ROWS:])

    locs[2].wait()
    result(0)
    for o in range(1, E):
        arrived(grd_out, grd_in, gs_sem, gr_sem, o).wait_recv()
    unpack(grd_in, gs)
    for h in range(2):
        for j in range(2):
            down_arrived(j, h).wait_recv()
            if h == 1:
                relay(2, j).start()
        result(1 + 2 * h)
        result(2 + 2 * h)

    def add_grad(b):
        hid_grad[...] += dot(gs[b], wd[b], NT)

    hid_grad[...] = jnp.zeros_like(hid_grad)
    for b in (dp, xp, yp):
        add_grad(b)
    for j in range(2):
        relay_arrived(2, j).wait_recv()
    result(LAST - 1)
    res_out[:, pl.ds(XROW, 16), :] = ext_sum[...].astype(BF).reshape(E, 16, CB)
    for o in range(1, E):
        back(res_out, res_in, os_sem, or_sem, LAST, o, XROW, 16, lax.rem(me + o, E), me).start()
    res_in[pl.ds(me, 1)] = res_out[pl.ds(me, 1)]
    add_grad(dg)

    gp = gate_pre[...]
    up = up_pre[...]
    hg = hid_grad[...]
    sg = jax.nn.sigmoid(gp)
    pre_gate[...] = (hg * up * sg * (1.0 + gp * (1.0 - sg))).astype(BF)
    pre_up[...] = (hg * gp * sg).astype(BF)
    ext = jnp.zeros((EXT, CB), F32)
    for b in range(NB):
        grad = (dot(pre_gate[...], wg[b], NT) + dot(pre_up[...], wu[b], NT)).astype(BF)
        ig_out[:, pl.ds(b * MAIN, MAIN), :] = grad[:ROWS].reshape(E, MAIN, CB)
        ext = ext + dot(fold(b), grad[ROWS:])
        size = MAIN
        if b == NB - 1:
            ig_out[:, pl.ds(XROW, 16), :] = ext.astype(BF).reshape(E, 16, CB)
            size = MAIN + 16
        for o in range(1, E):
            to = lax.rem(me + o, E)
            for i in ((0, 1, 2), (3, 4), (5,), ())[b]:
                back_out(i, o, to, me).wait_send()
            if b == 2:
                back(res_out, res_in, os_sem, or_sem, LAST, o, XROW, 16, to, me).wait_send()
            if b == 3:
                back(ig_out, ig_in, is_sem, ir_sem, 0, o, 0, MAIN, to, me).wait_send()
        for o in range(1, E):
            back(ig_out, ig_in, is_sem, ir_sem, b, o, b * MAIN, size, lax.rem(me + o, E), me).start()
    ig_in[pl.ds(me, 1)] = ig_out[pl.ds(me, 1)]

    for i in range(LAST):
        for o in range(1, E):
            frm = lax.rem(me + E - o, E)
            back_out(i, o, frm, frm).wait_recv()
    for o in range(1, E):
        frm = lax.rem(me + E - o, E)
        back(res_out, res_in, os_sem, or_sem, LAST, o, XROW, 16, frm, frm).wait_recv()

    def pairs(box, b, ext):
        rows = box[:, pl.ds(b * MAIN, MAIN), :].reshape(ROWS, CB)
        return [dot(p_main[k], rows) + dot(p_ext[k, b], ext) for k in range(2)]

    ext = res_in[:, pl.ds(XROW, 16), :].reshape(EXT, CB)
    dots = [jnp.zeros((T, 1), F32) for _ in range(2)]
    for b in range(NB):
        cols = slice(b * CB, (b + 1) * CB)
        two = pairs(res_in, b, ext)
        cot = cot_ref[:, cols].astype(F32)
        lo_ref[:, cols] = (gates[0] * two[0] + gates[1] * two[1]).astype(BF)
        dots = [dots[k] + jnp.sum(cot * two[k], axis=1, keepdims=True) for k in range(2)]
    lane = lax.broadcasted_iota(jnp.int32, (T, 8), 1)
    gg_ref[...] = jnp.where(lane == 0, dots[0], jnp.where(lane == 1, dots[1], 0.0)).T[0:2, :]

    both = p_main[0] + p_main[1]
    for b in range(NB):
        size = MAIN + 16 if b == NB - 1 else MAIN
        for o in range(1, E):
            frm = lax.rem(me + E - o, E)
            back(ig_out, ig_in, is_sem, ir_sem, b, o, b * MAIN, size, frm, frm).wait_recv()
        rows = ig_in[:, pl.ds(b * MAIN, MAIN), :].reshape(ROWS, CB)
        if b < NB - 1:
            ig_sum[b] = dot(both, rows)
        else:
            ext = ig_in[:, pl.ds(XROW, 16), :].reshape(EXT, CB)
            tg_ref[:, b * CB :] = (dot(both, rows) + dot(p_ext[0, b] + p_ext[1, b], ext)).astype(BF)
    for b in range(NB - 1):
        total = ig_sum[b] + dot(p_ext[0, b] + p_ext[1, b], ext)
        tg_ref[:, b * CB : (b + 1) * CB] = total.astype(BF)

    for j in range(2):
        for m in range(3):
            relay(m, j).wait_send()
        for m in range(2):
            own(m, j).wait_send()
            down(j, m).wait_send()
    for o in range(1, E):
        exchange(grd_out, grd_in, gs_sem, gr_sem, o).wait_send()
        to = lax.rem(me + o, E)
        for b in range(1, NB):
            size = MAIN + 16 if b == NB - 1 else MAIN
            back(ig_out, ig_in, is_sem, ir_sem, b, o, b * MAIN, size, to, me).wait_send()


def fused(MAIN, REM, tokens, routes, route_gates, w_gate, w_up, w_down, cotangent):
    E = lax.axis_size("expert")
    T, D = tokens.shape
    CB = D // 4
    FF = w_gate.shape[2]
    BOX = 4 * MAIN + 16
    R = E * (MAIN + REM)
    box = pltpu.VMEM((E, BOX, CB), BF)
    vm = pl.BlockSpec(memory_space=pltpu.VMEM)
    hb = pl.BlockSpec(memory_space=pl.ANY)
    dma = pltpu.SemaphoreType.DMA
    layer_out, token_grad, gate_grad = pl.pallas_call(
        functools.partial(moe_kernel, E, MAIN, REM),
        out_shape=(
            jax.ShapeDtypeStruct((T, D), BF),
            jax.ShapeDtypeStruct((T, D), BF),
            jax.ShapeDtypeStruct((2, T), F32),
        ),
        in_specs=[vm] * 4 + [hb] * 3,
        out_specs=(vm, vm, vm),
        scratch_shapes=[
            pltpu.VMEM((4, CB, FF), BF), pltpu.VMEM((4, CB, FF), BF), pltpu.VMEM((4, FF, CB), BF),
            box, box, box, box,
            box, box, box, box,
            pltpu.VMEM((4, R, CB), BF), pltpu.VMEM((4, R, CB), BF),
            pltpu.VMEM((E * MAIN, T), BF), pltpu.VMEM((16 // REM, E * 16, T), BF),
            pltpu.VMEM((2, T, E * MAIN), BF), pltpu.VMEM((2, 16 // REM, T, E * 16), BF),
            pltpu.VMEM((R, FF), F32), pltpu.VMEM((R, FF), F32), pltpu.VMEM((R, FF), F32),
            pltpu.VMEM((R, FF), BF), pltpu.VMEM((R, FF), BF), pltpu.VMEM((R, FF), BF), pltpu.VMEM((E * 16, CB), F32), pltpu.VMEM((3, T, CB), F32),
            dma((3,)), dma((3, 4)), dma((3, 4)), dma((2, 2)), dma((2, 2)),
            dma((E,)), dma((E,)), dma((E,)), dma((E,)),
            dma((7, E)), dma((7, E)), dma((4, E)), dma((4, E)),
        ],
        compiler_params=pltpu.CompilerParams(
            collective_id=0, has_side_effects=True, vmem_limit_bytes=56 * 1024 * 1024
        ),
    )(tokens, cotangent, routes.T, route_gates.T, w_gate, w_up, w_down)
    return layer_out, token_grad, gate_grad.T


def gather(x, axis):
    n = lax.axis_size("dp")
    me = lax.axis_index("dp")
    width = x.shape[axis]
    shape = list(x.shape)
    shape[axis] = n * width
    full = lax.dynamic_update_slice_in_dim(jnp.zeros(shape, x.dtype), x, me * width, axis)
    part = x
    for step in range(1, n):
        part = lax.ppermute(part, "dp", [(i, (i + 1) % n) for i in range(n)])
        full = lax.dynamic_update_slice_in_dim(full, part, lax.rem(me - step + n, n) * width, axis)
    return full


def general(capacity, tokens, routes, route_gates, w_gate, w_up, w_down, cotangent):
    groups = lax.axis_size("expert")
    tok_rows, width = tokens.shape
    top_count = routes.shape[1]
    pair_expert = routes.reshape(-1)
    pair_token = jnp.arange(tok_rows * top_count, dtype=jnp.int32) // top_count
    onehot = (pair_expert[:, None] == jnp.arange(groups, dtype=jnp.int32)[None, :]).astype(F32)
    before = (pair_token.size, pair_token.size)
    before = lax.broadcasted_iota(jnp.int32, before, 0) > lax.broadcasted_iota(jnp.int32, before, 1)
    slot_rank = jnp.sum(dot(before.astype(F32), onehot) * onehot, axis=1).astype(jnp.int32)
    slot_place = pair_expert * capacity + slot_rank
    pair_gate = route_gates.reshape(-1)
    cot_pairs = cotangent[pair_token].astype(F32)
    row_grad = (pair_gate[:, None] * cot_pairs).astype(BF)

    def send(rows):
        box = jnp.zeros((groups * capacity, width), BF).at[slot_place].set(rows)
        return swap(box.reshape(groups, capacity, width)).reshape(groups * capacity, width)

    def swap(box):
        return lax.all_to_all(box, "expert", split_axis=0, concat_axis=0, tiled=True)

    def fetch(rows):
        back = swap(rows.astype(BF).reshape(groups, capacity, width))
        return back.reshape(groups * capacity, width)[slot_place].astype(F32)

    gate_full, up_full, down_full = gather(w_gate[0], 0), gather(w_up[0], 0), gather(w_down[0], 1)
    x = send(tokens[pair_token])
    gate_pre, up_pre = dot(x, gate_full), dot(x, up_full)
    sg = jax.nn.sigmoid(gate_pre)
    pair_out = fetch(dot((gate_pre * sg * up_pre).astype(BF), down_full))
    hid_grad = dot(send(row_grad), down_full, NT)
    pre_gate = (hid_grad * up_pre * sg * (1.0 + gate_pre * (1.0 - sg))).astype(BF)
    pre_up = (hid_grad * gate_pre * sg).astype(BF)
    pair_grad = fetch(dot(pre_gate, gate_full, NT) + dot(pre_up, up_full, NT))
    layer_out = jnp.sum((pair_gate[:, None] * pair_out).reshape(tok_rows, top_count, width), axis=1).astype(BF)
    gate_grad = jnp.sum(cot_pairs * pair_out, axis=1).reshape(tok_rows, top_count)
    token_grad = jnp.sum(pair_grad.reshape(tok_rows, top_count, width), axis=1).astype(BF)
    return (layer_out, token_grad, gate_grad)


def local(tokens, routes, route_gates, w_gate, w_up, w_down, cotangent):
    groups = lax.axis_size("expert")
    args = (tokens, routes, route_gates, w_gate, w_up, w_down, cotangent)
    capacity = 9 * tokens.shape[0] * routes.shape[1] // (8 * groups)
    main = capacity // 16 * 16
    rem = capacity - main
    if lax.axis_size("dp") == 4 and main and rem == 4 and tokens.shape[1] % 512 == 0 and groups * main <= 512:
        return fused(main, rem, *args)
    return general(capacity, *args)


def solution(mesh):
    rows = P(("dp", "expert"), None)
    in_specs = (rows, rows, rows, P("expert", "dp", None), P("expert", "dp", None), P("expert", None, "dp"), rows)
    return jax.shard_map(local, mesh=mesh, in_specs=in_specs, out_specs=(rows, rows, rows), check_vma=False)
```

```python
import functools

import jax
import jax.numpy as jnp
from jax import lax
from jax.experimental import pallas as pl
from jax.experimental.pallas import tpu as pltpu
from jax.sharding import PartitionSpec as P

BF = jnp.bfloat16
F32 = jnp.float32
NN = (((1,), (0,)), ((), ()))
NT = (((1,), (1,)), ((), ()))


def dot(a, b, dims=NN):
    return lax.dot_general(a, b, dims, preferred_element_type=F32)


def moe_kernel(
    E,
    MAIN,
    REM,
    tok_ref, cot_ref, routes_t_ref, gates_t_ref,
    wg_ref, wu_ref, wd_ref,
    lo_ref, tg_ref, gg_ref,
    wg, wu, wd,
    tok_out, grd_out, tok_in, grd_in,
    res_out, res_in, ig_out, ig_in,
    xs, gs, s_main, s_ext, p_main, p_ext,
    gate_pre, up_pre, hid_grad, hidden, pre_gate, pre_up, ext_sum, ig_sum,
    loc_sem, ws_sem, wr_sem, ds_sem, dr_sem,
    ts_sem, tr_sem, gs_sem, gr_sem,
    os_sem, or_sem, is_sem, ir_sem,
):
    T = tok_ref.shape[0]
    NB = 4
    CB = tok_ref.shape[1] // NB
    FOLD = 16 // REM
    XROW = NB * MAIN
    EXT = E * 16
    UNF = E * REM
    ROWS = E * MAIN
    dp = lax.axis_index("dp")
    me = lax.axis_index("expert")
    xp = dp + 1 - 2 * lax.rem(dp, 2)
    yp = lax.rem(dp + 2, 4)
    dg = 3 - dp

    barrier = pltpu.get_barrier_semaphore()
    for o in range(1, 4):
        pl.semaphore_signal(barrier, inc=1, device_id={"dp": lax.rem(dp + o, 4)}, device_id_type=pl.DeviceIdType.MESH)
    for o in range(1, E):
        pl.semaphore_signal(barrier, inc=1, device_id={"expert": lax.rem(me + o, E)}, device_id_type=pl.DeviceIdType.MESH)
    pl.semaphore_wait(barrier, 3 + E - 1)

    mats = ((wg_ref, wg), (wu_ref, wu), (wd_ref, wd))

    def remote(src, dst, s, r, axis, to):
        return pltpu.make_async_remote_copy(
            src_ref=src, dst_ref=dst, send_sem=s, recv_sem=r, device_id={axis: to}, device_id_type=pl.DeviceIdType.MESH
        )

    def own(m, j):
        src, buf = mats[m]
        return remote(src.at[0], buf.at[dp], ws_sem.at[m, j], wr_sem.at[m, j], "dp", (xp, yp)[j])

    def own_arrived(m, j):
        src, buf = mats[m]
        b = (xp, yp)[j]
        return remote(src.at[0], buf.at[b], ws_sem.at[m, j], wr_sem.at[m, j], "dp", b)

    CUT = (CB + 255) // 256 * 128
    parts = ((0, CUT), (CUT, CB - CUT))

    def down(j, h):
        cols = pl.ds(*parts[h])
        return remote(wd_ref.at[0, :, cols], wd.at[dp, :, cols], ds_sem.at[j, h], dr_sem.at[j, h], "dp", (xp, yp)[j])

    def down_arrived(j, h):
        cols = pl.ds(*parts[h])
        b = (xp, yp)[j]
        return remote(wd_ref.at[0, :, cols], wd.at[b, :, cols], ds_sem.at[j, h], dr_sem.at[j, h], "dp", b)

    def relay(m, j):
        buf = mats[m][1]
        half = buf.shape[1] // 2
        b, to = ((xp, yp), (yp, xp))[j]
        part = buf.at[b, pl.ds(j * half, half)]
        return remote(part, part, ws_sem.at[m, 2 + j], wr_sem.at[m, 2 + j], "dp", to)

    def relay_arrived(m, j):
        buf = mats[m][1]
        half = buf.shape[1] // 2
        part = buf.at[dg, pl.ds(j * half, half)]
        return remote(part, part, ws_sem.at[m, 2 + j], wr_sem.at[m, 2 + j], "dp", (yp, xp)[j])

    for m in range(2):
        for j in range(2):
            own(m, j).start()
    locs = [pltpu.make_async_copy(src.at[0], buf.at[dp], loc_sem.at[m]) for m, (src, buf) in enumerate(mats)]
    for c in locs:
        c.start()

    r_t = routes_t_ref[...]
    g_t = gates_t_ref[...]
    row_e = lax.broadcasted_iota(jnp.int32, (E, T), 0)
    hit0 = r_t[0:1, :] == row_e
    hit1 = r_t[1:2, :] == row_e
    hit = jnp.logical_or(hit0, hit1)
    before = lax.broadcasted_iota(jnp.int32, (T, T), 0) < lax.broadcasted_iota(jnp.int32, (T, T), 1)
    rank_t = dot(jnp.where(hit, 1.0, 0.0).astype(BF), jnp.where(before, 1.0, 0.0).astype(BF)).astype(jnp.int32)
    rank_t = jnp.where(hit, rank_t, -1)
    gate_t = jnp.where(hit0, g_t[0:1, :], 0.0) + jnp.where(hit1, g_t[1:2, :], 0.0)
    row_m = lax.broadcasted_iota(jnp.int32, (MAIN, T), 0)
    row_x = lax.broadcasted_iota(jnp.int32, (16, T), 0)
    for e in range(E):
        rank_e = rank_t[e : e + 1, :]
        s_main[pl.ds(e * MAIN, MAIN), :] = jnp.where(row_m == rank_e, 1.0, 0.0).astype(BF)
        for q in range(FOLD):
            sel = jnp.logical_and(
                row_x - q * REM + MAIN == rank_e,
                jnp.logical_and(rank_e >= MAIN, jnp.logical_and(row_x >= q * REM, row_x < q * REM + REM)),
            )
            s_ext[q, pl.ds(e * 16, 16), :] = jnp.where(sel, 1.0, 0.0).astype(BF)

    def pack(src_ref, box, scale, scale_x):
        ext = jnp.zeros((EXT, CB), F32)
        for b in range(NB):
            block = src_ref[:, b * CB : (b + 1) * CB]
            rows = dot(s_main[...], block)
            if scale is not None:
                rows = rows * scale
            box[:, pl.ds(b * MAIN, MAIN), :] = rows.astype(BF).reshape(E, MAIN, CB)
            ext = ext + dot(s_ext[b], block)
        if scale is not None:
            ext = ext * scale_x
        box[:, pl.ds(XROW, 16), :] = ext.astype(BF).reshape(E, 16, CB)

    def exchange(src, dst, s, r, o):
        to = lax.rem(me + o, E)
        return remote(src.at[to], dst.at[me], s.at[o], r.at[o], "expert", to)

    def arrived(src, dst, s, r, o):
        frm = lax.rem(me + E - o, E)
        return remote(src.at[frm], dst.at[frm], s.at[o], r.at[o], "expert", frm)

    pack(tok_ref, tok_out, None, None)
    for o in range(1, E):
        exchange(tok_out, tok_in, ts_sem, tr_sem, o).start()
    tok_in[pl.ds(me, 1)] = tok_out[pl.ds(me, 1)]
    gsel, gsel_x = [], []
    for e in range(E):
        gate_e = gate_t[e : e + 1, :]
        sel = s_main[pl.ds(e * MAIN, MAIN), :].astype(F32)
        gsel.append(jnp.sum(sel * gate_e, axis=1, keepdims=True))
        sel = sum(s_ext[q, pl.ds(e * 16, 16), :].astype(F32) for q in range(FOLD))
        gsel_x.append(jnp.sum(sel * gate_e, axis=1, keepdims=True))
    pack(cot_ref, grd_out, jnp.concatenate(gsel, axis=0), jnp.concatenate(gsel_x, axis=0))
    for o in range(1, E):
        exchange(grd_out, grd_in, gs_sem, gr_sem, o).start()
    grd_in[pl.ds(me, 1)] = grd_out[pl.ds(me, 1)]

    ranks = rank_t.astype(F32)
    turned = [r_t[k : k + 1, :].astype(F32) for k in range(2)]
    turned += [jnp.sum(jnp.where(h, ranks, 0.0), axis=0, keepdims=True) for h in (hit0, hit1)]
    turned += [g_t[0:1, :], g_t[1:2, :], jnp.zeros((2, T), F32)]
    turned = jnp.concatenate(turned, axis=0).T
    gates = [turned[:, 4 + k : 5 + k] for k in range(2)]
    lane_m = lax.broadcasted_iota(jnp.int32, (T, ROWS), 1)
    lane_x = lax.broadcasted_iota(jnp.int32, (T, EXT), 1)
    for k in range(2):
        e_k = turned[:, k : k + 1].astype(jnp.int32)
        rk = turned[:, 2 + k : 3 + k].astype(jnp.int32)
        place = jnp.where(rk < MAIN, e_k * MAIN + rk, -1)
        p_main[k] = jnp.where(lane_m == place, 1.0, 0.0).astype(BF)
        for q in range(FOLD):
            place = jnp.where(rk >= MAIN, e_k * 16 + q * REM + rk - MAIN, -1)
            p_ext[k, q] = jnp.where(lane_x == place, 1.0, 0.0).astype(BF)

    for m in range(2):
        for j in range(2):
            own_arrived(m, j).wait_recv()
            relay(m, j).start()
    for h in range(2):
        for j in range(2):
            down(j, h).start()

    u_row = lax.broadcasted_iota(jnp.int32, (UNF, EXT), 0)
    u_col = lax.broadcasted_iota(jnp.int32, (UNF, EXT), 1)
    f_row = lax.broadcasted_iota(jnp.int32, (EXT, UNF), 0)
    f_col = lax.broadcasted_iota(jnp.int32, (EXT, UNF), 1)

    def unfold(q):
        same = (u_row // REM) * 16 + lax.rem(u_row, REM) + q * REM == u_col
        return jnp.where(same, 1.0, 0.0).astype(BF)

    def fold(q):
        same = (f_col // REM) * 16 + lax.rem(f_col, REM) + q * REM == f_row
        return jnp.where(same, 1.0, 0.0).astype(BF)

    def unpack(box, dst):
        ext = box[:, pl.ds(XROW, 16), :].reshape(EXT, CB)
        for b in range(NB):
            dst[b, pl.ds(0, ROWS), :] = box[:, pl.ds(b * MAIN, MAIN), :].reshape(ROWS, CB)
            dst[b, pl.ds(ROWS, UNF), :] = dot(unfold(b), ext).astype(BF)

    for o in range(1, E):
        arrived(tok_out, tok_in, ts_sem, tr_sem, o).wait_recv()
    unpack(tok_in, xs)
    locs[0].wait()
    locs[1].wait()

    def add_gate(b):
        gate_pre[...] += dot(xs[b], wg[b])

    def add_up(b):
        up_pre[...] += dot(xs[b], wu[b])

    gate_pre[...] = dot(xs[dp], wg[dp])
    up_pre[...] = dot(xs[dp], wu[dp])
    for b in (xp, yp):
        add_gate(b)
        add_up(b)
    for j in range(2):
        relay_arrived(0, j).wait_recv()
    add_gate(dg)
    for j in range(2):
        relay_arrived(1, j).wait_recv()
    add_up(dg)
    gp = gate_pre[...]
    hidden[...] = (gp * jax.nn.sigmoid(gp) * up_pre[...]).astype(BF)

    def back(src, dst, s, r, i, o, start, size, to, at):
        part = pl.ds(start, size)
        return remote(src.at[to, part], dst.at[at, part], s.at[i, o], r.at[i, o], "expert", to)

    steps = [(dp, 0, CB)] + [(b, *part) for part in parts for b in (xp, yp)] + [(dg, 0, CB)]
    LAST = len(steps)

    def back_out(i, o, to, at):
        b, first, width = steps[i]
        part = (pl.ds(pl.multiple_of(b * MAIN, MAIN), MAIN), pl.ds(first, width))
        return remote(
            res_out.at[(to, *part)], res_in.at[(at, *part)], os_sem.at[i, o], or_sem.at[i, o], "expert", to
        )

    ext_sum[...] = jnp.zeros_like(ext_sum)

    def result(i):
        b, first, width = steps[i]
        cols = slice(first, first + width)
        out = dot(hidden[...], wd[b, :, cols]).astype(BF)
        start = pl.multiple_of(b * MAIN, MAIN)
        res_out[:, pl.ds(start, MAIN), cols] = out[:ROWS].reshape(E, MAIN, width)
        for o in range(1, E):
            back_out(i, o, lax.rem(me + o, E), me).start()
        ext_sum[:, cols] += dot(fold(b), out[ROWS:])

    locs[2].wait()
    result(0)
    for o in range(1, E):
        arrived(grd_out, grd_in, gs_sem, gr_sem, o).wait_recv()
    unpack(grd_in, gs)
    for h in range(2):
        for j in range(2):
            down_arrived(j, h).wait_recv()
            if h == 1:
                relay(2, j).start()
        result(1 + 2 * h)
        result(2 + 2 * h)

    def add_grad(b):
        hid_grad[...] += dot(gs[b], wd[b], NT)

    hid_grad[...] = jnp.zeros_like(hid_grad)
    for b in (dp, xp, yp):
        add_grad(b)
    for j in range(2):
        relay_arrived(2, j).wait_recv()
    result(LAST - 1)
    res_out[:, pl.ds(XROW, 16), :] = ext_sum[...].astype(BF).reshape(E, 16, CB)
    for o in range(1, E):
        back(res_out, res_in, os_sem, or_sem, LAST, o, XROW, 16, lax.rem(me + o, E), me).start()
    res_in[pl.ds(me, 1)] = res_out[pl.ds(me, 1)]
    add_grad(dg)

    gp = gate_pre[...]
    up = up_pre[...]
    hg = hid_grad[...]
    sg = jax.nn.sigmoid(gp)
    pre_gate[...] = (hg * up * sg * (1.0 + gp * (1.0 - sg))).astype(BF)
    pre_up[...] = (hg * gp * sg).astype(BF)
    ext = jnp.zeros((EXT, CB), F32)
    for b in range(NB):
        grad = (dot(pre_gate[...], wg[b], NT) + dot(pre_up[...], wu[b], NT)).astype(BF)
        ig_out[:, pl.ds(b * MAIN, MAIN), :] = grad[:ROWS].reshape(E, MAIN, CB)
        ext = ext + dot(fold(b), grad[ROWS:])
        size = MAIN
        if b == NB - 1:
            ig_out[:, pl.ds(XROW, 16), :] = ext.astype(BF).reshape(E, 16, CB)
            size = MAIN + 16
        for o in range(1, E):
            back(ig_out, ig_in, is_sem, ir_sem, b, o, b * MAIN, size, lax.rem(me + o, E), me).start()
    ig_in[pl.ds(me, 1)] = ig_out[pl.ds(me, 1)]

    for i in range(LAST):
        for o in range(1, E):
            frm = lax.rem(me + E - o, E)
            back_out(i, o, frm, frm).wait_recv()
    for o in range(1, E):
        frm = lax.rem(me + E - o, E)
        back(res_out, res_in, os_sem, or_sem, LAST, o, XROW, 16, frm, frm).wait_recv()

    def pairs(box, b, ext):
        rows = box[:, pl.ds(b * MAIN, MAIN), :].reshape(ROWS, CB)
        return [dot(p_main[k], rows) + dot(p_ext[k, b], ext) for k in range(2)]

    ext = res_in[:, pl.ds(XROW, 16), :].reshape(EXT, CB)
    dots = [jnp.zeros((T, 1), F32) for _ in range(2)]
    for b in range(NB):
        cols = slice(b * CB, (b + 1) * CB)
        two = pairs(res_in, b, ext)
        cot = cot_ref[:, cols].astype(F32)
        lo_ref[:, cols] = (gates[0] * two[0] + gates[1] * two[1]).astype(BF)
        dots = [dots[k] + jnp.sum(cot * two[k], axis=1, keepdims=True) for k in range(2)]
    lane = lax.broadcasted_iota(jnp.int32, (T, 8), 1)
    gg_ref[...] = jnp.where(lane == 0, dots[0], jnp.where(lane == 1, dots[1], 0.0)).T[0:2, :]

    both = p_main[0] + p_main[1]
    for b in range(NB):
        size = MAIN + 16 if b == NB - 1 else MAIN
        for o in range(1, E):
            frm = lax.rem(me + E - o, E)
            back(ig_out, ig_in, is_sem, ir_sem, b, o, b * MAIN, size, frm, frm).wait_recv()
        rows = ig_in[:, pl.ds(b * MAIN, MAIN), :].reshape(ROWS, CB)
        if b < NB - 1:
            ig_sum[b] = dot(both, rows)
        else:
            ext = ig_in[:, pl.ds(XROW, 16), :].reshape(EXT, CB)
            tg_ref[:, b * CB :] = (dot(both, rows) + dot(p_ext[0, b] + p_ext[1, b], ext)).astype(BF)
    for b in range(NB - 1):
        total = ig_sum[b] + dot(p_ext[0, b] + p_ext[1, b], ext)
        tg_ref[:, b * CB : (b + 1) * CB] = total.astype(BF)

    for j in range(2):
        for m in range(3):
            relay(m, j).wait_send()
        for m in range(2):
            own(m, j).wait_send()
            down(j, m).wait_send()
    for o in range(1, E):
        exchange(tok_out, tok_in, ts_sem, tr_sem, o).wait_send()
        exchange(grd_out, grd_in, gs_sem, gr_sem, o).wait_send()
        to = lax.rem(me + o, E)
        for i in range(LAST):
            back_out(i, o, to, me).wait_send()
        back(res_out, res_in, os_sem, or_sem, LAST, o, XROW, 16, to, me).wait_send()
        for b in range(NB):
            size = MAIN + 16 if b == NB - 1 else MAIN
            back(ig_out, ig_in, is_sem, ir_sem, b, o, b * MAIN, size, to, me).wait_send()


def fused(MAIN, REM, tokens, routes, route_gates, w_gate, w_up, w_down, cotangent):
    E = lax.axis_size("expert")
    T, D = tokens.shape
    CB = D // 4
    FF = w_gate.shape[2]
    BOX = 4 * MAIN + 16
    R = E * (MAIN + REM)
    box = pltpu.VMEM((E, BOX, CB), BF)
    vm = pl.BlockSpec(memory_space=pltpu.VMEM)
    hb = pl.BlockSpec(memory_space=pl.ANY)
    dma = pltpu.SemaphoreType.DMA
    layer_out, token_grad, gate_grad = pl.pallas_call(
        functools.partial(moe_kernel, E, MAIN, REM),
        out_shape=(
            jax.ShapeDtypeStruct((T, D), BF),
            jax.ShapeDtypeStruct((T, D), BF),
            jax.ShapeDtypeStruct((2, T), F32),
        ),
        in_specs=[vm] * 4 + [hb] * 3,
        out_specs=(vm, vm, vm),
        scratch_shapes=[
            pltpu.VMEM((4, CB, FF), BF), pltpu.VMEM((4, CB, FF), BF), pltpu.VMEM((4, FF, CB), BF),
            box, box, box, box,
            box, box, box, box,
            pltpu.VMEM((4, R, CB), BF), pltpu.VMEM((4, R, CB), BF),
            pltpu.VMEM((E * MAIN, T), BF), pltpu.VMEM((16 // REM, E * 16, T), BF),
            pltpu.VMEM((2, T, E * MAIN), BF), pltpu.VMEM((2, 16 // REM, T, E * 16), BF),
            pltpu.VMEM((R, FF), F32), pltpu.VMEM((R, FF), F32), pltpu.VMEM((R, FF), F32),
            pltpu.VMEM((R, FF), BF), pltpu.VMEM((R, FF), BF), pltpu.VMEM((R, FF), BF), pltpu.VMEM((E * 16, CB), F32), pltpu.VMEM((3, T, CB), F32),
            dma((3,)), dma((3, 4)), dma((3, 4)), dma((2, 2)), dma((2, 2)),
            dma((E,)), dma((E,)), dma((E,)), dma((E,)),
            dma((7, E)), dma((7, E)), dma((4, E)), dma((4, E)),
        ],
        compiler_params=pltpu.CompilerParams(
            collective_id=0, has_side_effects=True, vmem_limit_bytes=56 * 1024 * 1024
        ),
    )(tokens, cotangent, routes.T, route_gates.T, w_gate, w_up, w_down)
    return layer_out, token_grad, gate_grad.T


def gather(x, axis):
    n = lax.axis_size("dp")
    me = lax.axis_index("dp")
    width = x.shape[axis]
    shape = list(x.shape)
    shape[axis] = n * width
    full = lax.dynamic_update_slice_in_dim(jnp.zeros(shape, x.dtype), x, me * width, axis)
    part = x
    for step in range(1, n):
        part = lax.ppermute(part, "dp", [(i, (i + 1) % n) for i in range(n)])
        full = lax.dynamic_update_slice_in_dim(full, part, lax.rem(me - step + n, n) * width, axis)
    return full


def general(capacity, tokens, routes, route_gates, w_gate, w_up, w_down, cotangent):
    groups = lax.axis_size("expert")
    tok_rows, width = tokens.shape
    top_count = routes.shape[1]
    pair_expert = routes.reshape(-1)
    pair_token = jnp.arange(tok_rows * top_count, dtype=jnp.int32) // top_count
    onehot = (pair_expert[:, None] == jnp.arange(groups, dtype=jnp.int32)[None, :]).astype(F32)
    before = (pair_token.size, pair_token.size)
    before = lax.broadcasted_iota(jnp.int32, before, 0) > lax.broadcasted_iota(jnp.int32, before, 1)
    slot_rank = jnp.sum(dot(before.astype(F32), onehot) * onehot, axis=1).astype(jnp.int32)
    slot_place = pair_expert * capacity + slot_rank
    pair_gate = route_gates.reshape(-1)
    cot_pairs = cotangent[pair_token].astype(F32)
    row_grad = (pair_gate[:, None] * cot_pairs).astype(BF)

    def send(rows):
        box = jnp.zeros((groups * capacity, width), BF).at[slot_place].set(rows)
        return swap(box.reshape(groups, capacity, width)).reshape(groups * capacity, width)

    def swap(box):
        return lax.all_to_all(box, "expert", split_axis=0, concat_axis=0, tiled=True)

    def fetch(rows):
        back = swap(rows.astype(BF).reshape(groups, capacity, width))
        return back.reshape(groups * capacity, width)[slot_place].astype(F32)

    gate_full, up_full, down_full = gather(w_gate[0], 0), gather(w_up[0], 0), gather(w_down[0], 1)
    x = send(tokens[pair_token])
    gate_pre, up_pre = dot(x, gate_full), dot(x, up_full)
    sg = jax.nn.sigmoid(gate_pre)
    pair_out = fetch(dot((gate_pre * sg * up_pre).astype(BF), down_full))
    hid_grad = dot(send(row_grad), down_full, NT)
    pre_gate = (hid_grad * up_pre * sg * (1.0 + gate_pre * (1.0 - sg))).astype(BF)
    pre_up = (hid_grad * gate_pre * sg).astype(BF)
    pair_grad = fetch(dot(pre_gate, gate_full, NT) + dot(pre_up, up_full, NT))
    layer_out = jnp.sum((pair_gate[:, None] * pair_out).reshape(tok_rows, top_count, width), axis=1).astype(BF)
    gate_grad = jnp.sum(cot_pairs * pair_out, axis=1).reshape(tok_rows, top_count)
    token_grad = jnp.sum(pair_grad.reshape(tok_rows, top_count, width), axis=1).astype(BF)
    return (layer_out, token_grad, gate_grad)


def local(tokens, routes, route_gates, w_gate, w_up, w_down, cotangent):
    groups = lax.axis_size("expert")
    args = (tokens, routes, route_gates, w_gate, w_up, w_down, cotangent)
    capacity = 9 * tokens.shape[0] * routes.shape[1] // (8 * groups)
    main = capacity // 16 * 16
    rem = capacity - main
    if lax.axis_size("dp") == 4 and main and rem == 4 and tokens.shape[1] % 512 == 0 and groups * main <= 512:
        return fused(main, rem, *args)
    return general(capacity, *args)


def solution(mesh):
    rows = P(("dp", "expert"), None)
    in_specs = (rows, rows, rows, P("expert", "dp", None), P("expert", "dp", None), P("expert", None, "dp"), rows)
    return jax.shard_map(local, mesh=mesh, in_specs=in_specs, out_specs=(rows, rows, rows), check_vma=False)
```
